32 devices in a mesh: row: 8 (over y, x, core), col: 4 (over z).
Axes of the slice: x: 2, y: 2, z: 4, core: 2. Of those that a mesh axis runs over, the one named last changes fastest.
Arguments:
- noisy: float32 [2048, 4096], P('row', 'col'), may hold values from -6 to 6
- strength: float32 [2048, 4096], P('row', 'col'), may hold values from 0.1 to 1
Outputs:
- denoised: float32 [2048, 4096], P('row', 'col')
- dual: float32 [2, 2048, 4096], P(None, 'row', 'col')
The draws below stay inside these ranges and needn't reach their ends.
All inputs are finite; a program needn't handle non-finite values.
Results may differ from the reference program's by a relative error of at most 0.0003.
Values sent between devices are 32-bit elements; how exact they have to be, the bound alone decides.
A program may use at most 128 MiB of HBM per device.

```python
import math
import jax
import jax.numpy as jnp

LEVELS = 5
SWEEPS = 3
NX = 2048
NY = 4096


def levels(stream_key, dims, pieces, smallest, high):
    loudness = 1.0
    for axis_at, blocks in pieces:
        heights = jax.random.uniform(jax.random.fold_in(jax.random.fold_in(stream_key, 6), axis_at), (blocks,), jnp.float32, smallest / len(pieces), high / len(pieces))
        loudness = loudness * jnp.repeat(jnp.exp(heights), dims[axis_at] // blocks).reshape((-1,) + (1,) * (len(dims) - 1 - axis_at))
    return loudness


def gaussian(rng, dims, deviation, most, shards=(), held_as=jnp.bfloat16):
    entries = deviation * jax.random.normal(rng, dims, jnp.float32)
    if shards:
        entries = entries * levels(rng, dims, shards, -0.22, 0.18)
    return jnp.clip(entries, -most, most).astype(held_as)


def setup_inputs(seed: int = 0) -> dict:
    key_list = jax.random.split(jax.random.key(seed), 3)
    noisy = gaussian(key_list[0], (NX, NY), 1.0, 6.0, ((0, 8), (1, 4)), jnp.float32)
    strength = jnp.clip(jnp.exp(math.log(1.0) - 2.3025851 * jax.random.uniform(key_list[1], (NX, NY), jnp.float32) ** levels(key_list[1], (NX, NY), ((0, 8), (1, 4)), -0.2, 0.2)), 0.1, 1.0)
    return {"noisy": noisy, "strength": strength}


primal_step = 0.25
dual_step = 0.5
relax_weight = 0.8
damping = 0.01

def widen_zero(values):
    return jnp.pad(values, 1)

def operate(values, widen, centre):
    padded = widen(values)
    beside_all = padded[2:, 1:-1] + padded[:-2, 1:-1] + padded[1:-1, 2:] + padded[1:-1, :-2]
    return centre * values - beside_all

def relax(values, source, widen, centre):
    return values + relax_weight * (source - operate(values, widen, centre)) / centre

def restrict(values):
    paired = values[0::2] + values[1::2]
    return paired[:, 0::2] + paired[:, 1::2]

def prolong(padded):
    middle = padded[1:-1, 1:-1]
    row_total = middle.shape[0] * 2
    col_total = middle.shape[1] * 2
    even_rows = (jnp.arange(row_total) % 2 == 0)[:, None]
    even_cols = (jnp.arange(col_total) % 2 == 0)[None, :]

    def spread(piece):
        return jnp.repeat(jnp.repeat(piece, 2, axis=0), 2, axis=1)
    vertical = jnp.where(even_rows, spread(padded[:-2, 1:-1]), spread(padded[2:, 1:-1]))
    sideways = jnp.where(even_cols, spread(padded[1:-1, :-2]), spread(padded[1:-1, 2:]))
    upper_diag = jnp.where(even_cols, spread(padded[:-2, :-2]), spread(padded[:-2, 2:]))
    lower_diag = jnp.where(even_cols, spread(padded[2:, :-2]), spread(padded[2:, 2:]))
    diagonal = jnp.where(even_rows, upper_diag, lower_diag)
    return 0.5625 * spread(middle) + 0.1875 * vertical + 0.1875 * sideways + 0.0625 * diagonal

def cycle(grid_level, source, widen, descend):
    centre = 4.0 + damping * 4.0 ** grid_level
    values = relax_weight * source / centre
    for repeat in range(SWEEPS - 1):
        values = relax(values, source, widen, centre)
    if grid_level == LEVELS - 1:
        return values
    remainder = source - operate(values, widen, centre)
    values = values + prolong(descend(grid_level + 1, restrict(remainder)))
    for repeat in range(SWEEPS):
        values = relax(values, source, widen, centre)
    return values

def descend_local(grid_level, source):
    return widen_zero(cycle(grid_level, source, widen_zero, descend_local))

def primal_dual(primal, extrap, dual_rows, dual_cols, noisy, strength):
    total_rows, total_cols = extrap.shape
    row_index = jnp.arange(total_rows)[:, None]
    col_index = jnp.arange(total_cols)[None, :]
    below = jnp.concatenate([extrap[1:], jnp.zeros((1, total_cols), extrap.dtype)], axis=0)
    beside = jnp.concatenate([extrap[:, 1:], jnp.zeros((total_rows, 1), extrap.dtype)], axis=1)
    grad_rows = jnp.where(row_index < total_rows - 1, below - extrap, 0.0)
    grad_cols = jnp.where(col_index < total_cols - 1, beside - extrap, 0.0)
    step_rows = dual_rows + dual_step * grad_rows
    step_cols = dual_cols + dual_step * grad_cols
    shrink = strength / jnp.maximum(strength, jnp.sqrt(step_rows * step_rows + step_cols * step_cols))
    new_rows = step_rows * shrink
    new_cols = step_cols * shrink
    above = jnp.concatenate([jnp.zeros((1, total_cols), extrap.dtype), new_rows[:-1]], axis=0)
    leftward = jnp.concatenate([jnp.zeros((total_rows, 1), extrap.dtype), new_cols[:, :-1]], axis=1)
    across = jnp.where(row_index < total_rows - 1, new_rows, 0.0) - jnp.where(row_index > 0, above, 0.0)
    along = jnp.where(col_index < total_cols - 1, new_cols, 0.0) - jnp.where(col_index > 0, leftward, 0.0)
    divergence = across + along
    updated = (primal + primal_step * (divergence + noisy)) / (1.0 + primal_step)
    return (updated, new_rows, new_cols, divergence)

def reference(noisy, strength):
    blank = jnp.zeros_like(noisy)
    primal, dual_rows, dual_cols, divergence = primal_dual(noisy, noisy, blank, blank, noisy, strength)
    remainder = noisy + divergence - primal
    correction = cycle(0, remainder, widen_zero, descend_local)
    primal = primal + correction
    primal, dual_rows, dual_cols, divergence = primal_dual(primal, primal, dual_rows, dual_cols, noisy, strength)
    return (primal, jnp.stack([dual_rows, dual_cols]))
```

```python
from functools import partial

import jax
import jax.numpy as jnp
from jax import lax
from jax.experimental import pallas as pl
from jax.experimental.pallas import tpu as pltpu
from jax.sharding import PartitionSpec as P

F32 = jnp.float32
BF16 = jnp.bfloat16
MESH = pl.DeviceIdType.MESH
VMEM = pltpu.VMEM

damping = 0.01
GUARD = 8
HALO0 = 8
HALO1 = 72
DIRECTIONS = ((-1, 0), (1, 0), (0, -1), (0, 1), (-1, -1), (-1, 1), (1, -1), (1, 1))
VMEM_LIMIT = 58 * 1024 * 1024


def centre(level):
    return 4.0 + damping * 4.0**level


def iota(shape, dim):
    return lax.broadcasted_iota(jnp.int32, shape, dim)


def west(x):
    return pltpu.roll(x, 1, 1)


def east(x):
    return pltpu.roll(x, x.shape[1] - 1, 1)


def north(x):
    return pltpu.roll(x, 1, 0)


def south(x):
    return pltpu.roll(x, x.shape[0] - 1, 0)


def split(x):
    high = x.astype(BF16)
    return high, (x - high.astype(F32)).astype(BF16)


def times(x, matrix):
    high, low = split(x)
    return jnp.dot(high, matrix, preferred_element_type=F32) + jnp.dot(
        low, matrix, preferred_element_type=F32
    )


def apply_rows(matrix, x):
    high, low = split(x)
    return jnp.dot(matrix, high, preferred_element_type=F32) + jnp.dot(
        matrix, low, preferred_element_type=F32
    )


def as_matrix(mask):
    return jnp.where(mask, 1.0, 0.0).astype(BF16)


def pair_rows(coarse, fine):
    return as_matrix((iota((coarse, fine), 1) >> 1) == iota((coarse, fine), 0))


def pair_cols():
    return as_matrix((iota((256, 128), 0) >> 1) == iota((256, 128), 1))


def pair_cols_tail():
    i = iota((128, 128), 0)
    return as_matrix((i >> 1) + jnp.where(i >= 64, 64, 0) == iota((128, 128), 1))


def interleave():
    i = iota((256, 256), 0)
    return as_matrix(2 * (i & 127) + (i >> 7) == iota((256, 256), 1))


def interleave_tail():
    i = iota((256, 128), 0)
    n = iota((256, 128), 1)
    return as_matrix(2 * (i & 127) + (i >> 7) == n + jnp.where(n >= 64, 128, 0))


def spread_rows(fine, coarse, offset):
    f = iota((fine, coarse), 0)
    k = iota((fine, coarse), 1)
    near = (f >> 1) + offset
    far = near + 2 * (f & 1) - 1
    return (jnp.where(k == near, 0.75, 0.0) + jnp.where(k == far, 0.25, 0.0)).astype(BF16)


def spread_cols(c):
    return 0.75 * c + 0.25 * west(c), 0.75 * c + 0.25 * east(c)


def joined(even, odd, block):
    at = slice(128 * block, 128 * block + 128)
    return jnp.concatenate([even[:, at], odd[:, at]], axis=1)


def col_index(width, own, right):
    lane = iota((1, width), 1)
    return lax.axis_index("col") * own + jnp.where(lane < own + right, lane, lane - width)


def col_inside(width, own, right):
    g = col_index(width, own, right)
    return (g >= 0) & (g < own * lax.axis_size("col"))


def row_inside(count, own, halo):
    g = lax.axis_index("row") * own - halo + iota((count, 1), 0)
    return (g >= 0) & (g < own * lax.axis_size("row"))


def weights(level, count, width, own_rows, own_cols, halo, right):
    inside = row_inside(count, own_rows, halo) & col_inside(width, own_cols, right)
    return jnp.where(inside, 0.8 / centre(level), 0.0)


def neighbour_exists(drow, dcol):
    row = lax.axis_index("row") + drow
    col = lax.axis_index("col") + dcol
    return (
        (row >= 0) & (row < lax.axis_size("row")) & (col >= 0) & (col < lax.axis_size("col"))
    )


def exchange(sources, targets, send_sem, recv_sem):
    barrier = pltpu.get_barrier_semaphore()
    row, col = lax.axis_index("row"), lax.axis_index("col")
    for drow, dcol in DIRECTIONS:

        @pl.when(neighbour_exists(drow, dcol))
        def _():
            pl.semaphore_signal(
                barrier, inc=1, device_id=(row + drow, col + dcol), device_id_type=MESH
            )

    pl.semaphore_wait(
        barrier, sum(jnp.where(neighbour_exists(*d), 1, 0) for d in DIRECTIONS)
    )

    def copy(d):
        drow, dcol = DIRECTIONS[d]
        return pltpu.make_async_remote_copy(
            src_ref=sources[d],
            dst_ref=targets[d],
            send_sem=send_sem.at[d],
            recv_sem=recv_sem.at[d],
            device_id=(row + drow, col + dcol),
            device_id_type=MESH,
        )

    order = (2, 3, 4, 5, 6, 7, 0, 1)
    for d in order:

        @pl.when(neighbour_exists(*DIRECTIONS[d]))
        def _():
            copy(d).start()

    for d in order:
        drow, dcol = DIRECTIONS[d]

        @pl.when(neighbour_exists(drow, dcol))
        def _():
            copy(d).wait_send()

        @pl.when(neighbour_exists(-drow, -dcol))
        def _():
            copy(d).wait_recv()


def exchange_image(
    noisy, strength, *rest
):
    targets, scratch = rest[:8], rest[8:]
    vertical, sides, corners, send_sem, recv_sem = scratch
    rows, cols = noisy.shape
    lane = iota((16, 128), 1)
    for k, ref in enumerate((noisy, strength)):
        at = slice(8 * k, 8 * k + 8)
        vertical[0, at] = ref[0:8, :]
        vertical[1, at] = ref[rows - 8 : rows, :]
        corners[0, at] = ref[0:8, 0:128]
        corners[1, at] = ref[0:8, cols - 128 : cols]
        corners[2, at] = ref[rows - 8 : rows, 0:128]
        corners[3, at] = ref[rows - 8 : rows, cols - 128 : cols]
        first = jnp.zeros((16, 128), F32)
        last = jnp.zeros((16, 128), F32)
        for g in range(16):
            here = (lane >= 8 * g) & (lane < 8 * g + 8)
            near = slice(16 * g, 16 * g + 16)
            first = jnp.where(here, pltpu.roll(ref[near, 0:128], 8 * g, 1), first)
            last = jnp.where(
                here, pltpu.roll(ref[near, cols - 128 : cols], (8 * g + 8) % 128, 1), last
            )
        sides[0, 16 * k : 16 * k + 16] = first
        sides[1, 16 * k : 16 * k + 16] = last
    sources = (
        vertical.at[0],
        vertical.at[1],
        sides.at[0],
        sides.at[1],
        corners.at[0],
        corners.at[1],
        corners.at[2],
        corners.at[3],
    )
    exchange(sources, targets, send_sem, recv_sem)


def exchange_source(source, *rest):
    targets, (send_sem, recv_sem) = rest[:8], rest[8:]
    rows, cols = source.shape
    up, down = pl.ds(0, HALO1), pl.ds(rows - HALO1, HALO1)
    left, right = pl.ds(0, 128), pl.ds(cols - 128, 128)
    sources = (
        source.at[up, :],
        source.at[down, :],
        source.at[:, left],
        source.at[:, right],
        source.at[up, left],
        source.at[up, right],
        source.at[down, left],
        source.at[down, right],
    )
    exchange(sources, targets, send_sem, recv_sem)


def tile_valid(tile, own, halo):
    g = lax.axis_index("row") * own - halo + tile * 8
    return jnp.where((g >= 0) & (g < own * lax.axis_size("row")), 1.0, 0.0)


def neighbours(ref, start):
    x = ref[pl.ds(start, 24), :]
    middle = x[8:16]
    return middle, (x[7:15] + x[9:17]) + (west(middle) + east(middle))


def for_tiles(first, last, body, unroll=2):
    def step(tile, carry):
        body(tile, pl.multiple_of(tile * 8, 8))
        return carry

    lax.fori_loop(first, last, step, 0, unroll=unroll)


def sweep(old, new, source, gain, own, halo, tiles):
    def body(tile, start):
        middle, beside = neighbours(old, start)
        k = gain * tile_valid(tile, own, halo)
        new[pl.ds(start + 8, 8), :] = 0.2 * middle + k * (source[pl.ds(start + 8, 8), :] + beside)

    for_tiles(0, tiles, body)


def first_sweep(new, source, gain, own, halo, tiles):
    def body(tile, start):
        k = gain * tile_valid(tile, own, halo)
        new[pl.ds(start + 8, 8), :] = k * source[pl.ds(start + 8, 8), :]

    for_tiles(0, tiles, body)


def dual_masks(tile, own_rows, width, own_cols, halo, right):
    g = lax.axis_index("row") * own_rows - halo + tile * 8 + iota((8, 1), 0)
    return jnp.where((g >= 0) & (g < own_rows * lax.axis_size("row") - 1), 1.0, 0.0)


def shrunk(qa, qb, bound):
    shrink = jnp.minimum(1.0, bound * lax.rsqrt(qa * qa + qb * qb))
    return qa * shrink, qb * shrink


def clear_guards(ref):
    rows, width = ref.shape
    ref[0:GUARD, :] = jnp.zeros((GUARD, width), ref.dtype)
    ref[rows - GUARD : rows, :] = jnp.zeros((GUARD, width), ref.dtype)


def half_cols_mask(width, own, right):
    g = col_index(width, own, right)
    return jnp.where((g >= 0) & (g < own * lax.axis_size("col") - 1), 0.5, 0.0)


def down_level0(
    noisy, strength, up, down, left, right, upleft, upright, downleft, downright,
    wide_noisy, wide_strength, dual_a, dual_b, source, values, coarse, other,
):
    rows, cols = noisy.shape
    width = wide_noisy.shape[1]
    total = wide_noisy.shape[0]
    tiles = (total - 2 * GUARD) // 8
    lane = iota((16, 128), 1)
    right_end = jnp.where(neighbour_exists(0, 1), 8, 0)
    left_start = jnp.where(neighbour_exists(0, -1), 120, 128)
    top = GUARD + HALO0
    for k, (ref, wide, fill) in enumerate(((noisy, wide_noisy, 0.0), (strength, wide_strength, 1.0))):
        wide[top : top + rows, 0:cols] = ref[...]
        wide[0:top, :] = jnp.full((top, width), fill, F32)
        wide[top + rows : total, :] = jnp.full((total - top - rows, width), fill, F32)
        from_right = right[16 * k : 16 * k + 16]
        from_left = left[16 * k : 16 * k + 16]
        for g in range(16):
            piece = jnp.where(
                lane < right_end,
                pltpu.roll(from_right, (128 - 8 * g) % 128, 1),
                jnp.where(lane >= left_start, pltpu.roll(from_left, (120 - 8 * g) % 128, 1), fill),
            )
            wide[top + 16 * g : top + 16 * g + 16, cols:width] = piece
        at = slice(8 * k, 8 * k + 8)
        lane8 = lane[0:8]
        for edge, other_left, other_right, drow, place in (
            (up, upleft, upright, -1, GUARD),
            (down, downleft, downright, 1, top + rows),
        ):

            @pl.when(neighbour_exists(drow, 0))
            def _():
                wide[place : place + 8, 0:cols] = edge[at, :]
                wide[place : place + 8, cols:width] = jnp.where(
                    lane8 < right_end,
                    other_right[at, :],
                    jnp.where(lane8 >= left_start, other_left[at, :], fill),
                )

    for ref in (dual_a, dual_b, source, values, other):
        clear_guards(ref)

    inside = col_inside(width, cols, 64)
    gain = jnp.where(inside, 0.8 / centre(0), 0.0)
    half_cols = half_cols_mask(width, cols, 64)

    def first_step(tile, start):
        x = wide_noisy[pl.ds(start + 8, 16), :]
        w = x[0:8]
        half_rows = 0.5 * dual_masks(tile, rows, width, cols, HALO0, 64)
        qa = half_rows * (x[1:9] - w)
        qb = half_cols * (east(w) - w)
        a, b = shrunk(qa, qb, wide_strength[pl.ds(start + 8, 8), :])
        dual_a[pl.ds(start + 8, 8), :] = a
        dual_b[pl.ds(start + 8, 8), :] = b
        above = dual_a[pl.ds(start, 16), :][7:15]
        s = 0.8 * ((a - above) + (b - west(b)))
        source[pl.ds(start + 8, 8), :] = s
        other[pl.ds(start + 8, 8), :] = (gain * tile_valid(tile, rows, HALO0)) * s

    for_tiles(0, tiles, first_step, unroll=1)
    sweep(other, values, source, gain, rows, HALO0, tiles)
    sweep(values, other, source, gain, rows, HALO0, tiles)

    def residual(tile, start):
        middle, beside = neighbours(other, start)
        values[pl.ds(start + 8, 8), :] = (
            source[pl.ds(start + 8, 8), :] - centre(0) * middle + beside
        )

    for_tiles(1, tiles - 1, residual)
    rows_matrix = pair_rows(rows // 2, rows)
    cols_matrix = pair_cols()
    for block in range(cols // 256):
        piece = values[top : top + rows, 256 * block : 256 * block + 256]
        coarse[:, 128 * block : 128 * block + 128] = times(
            apply_rows(rows_matrix, piece), cols_matrix
        )

    def back(tile, start):
        values[pl.ds(start + 8, 8), :] = other[pl.ds(start + 8, 8), :]

    for_tiles(0, tiles, back)


def relax(e, source, gain):
    beside = (north(e) + south(e)) + (west(e) + east(e))
    return 0.2 * e + gain * (source + beside)


def smoothed(source, gain):
    e = gain * source
    e = relax(e, source, gain)
    return relax(e, source, gain)


def remaining(e, source, level):
    return source - centre(level) * e + ((north(e) + south(e)) + (west(e) + east(e)))


def coarse_levels(source2, own_rows, own_cols):
    n2, n3, n4 = 144, 80, 48
    gain2 = weights(2, n2, own_cols + 128, own_rows, own_cols, 36, 64)
    gain3 = weights(3, n3, 256, own_rows // 2, own_cols // 2, 18, 64)
    gain4 = weights(4, n4, 128, own_rows // 4, own_cols // 4, 9, 32)
    spread, spread_tail = interleave(), interleave_tail()
    pairs, pairs_tail = pair_cols(), pair_cols_tail()

    e2 = smoothed(source2, gain2)
    left = apply_rows(pair_rows(n3, n2), remaining(e2, source2, 2))
    source3 = jnp.concatenate(
        [times(left[:, 0:256], pairs), times(left[:, 256:384], pairs_tail)], axis=1
    )
    e3 = smoothed(source3, gain3)
    source4 = times(apply_rows(pair_rows(n4, n3), remaining(e3, source3, 3)), pairs)
    e4 = smoothed(source4, gain4)

    even, odd = spread_cols(e4)
    wide = times(joined(even, odd, 0), spread)
    e3 = e3 + apply_rows(spread_rows(n3, n4, 0), wide)
    e3 = jnp.where(gain3 > 0.0, e3, 0.0)
    for _ in range(3):
        e3 = relax(e3, source3, gain3)

    even, odd = spread_cols(e3)
    wide = jnp.concatenate(
        [times(joined(even, odd, 0), spread), times(joined(even, odd, 1), spread_tail)], axis=1
    )
    e2 = e2 + apply_rows(spread_rows(n2, n3, 0), wide)
    e2 = jnp.where(gain2 > 0.0, e2, 0.0)
    for _ in range(3):
        e2 = relax(e2, source2, gain2)
    return e2


def up_levels(
    coarse, up, down, left, right, upleft, upright, downleft, downright,
    wide_noisy, wide_strength, dual_a, dual_b, source, values,
    image, dual,
    source1, one, two, other, new_a,
):
    rows1, cols1 = coarse.shape
    width1 = cols1 + 256
    tiles1 = (source1.shape[0] - 2 * GUARD) // 8
    top1 = GUARD + HALO1
    source1[...] = jnp.zeros(source1.shape, F32)
    for ref in (one, two, other, new_a):
        clear_guards(ref)
    source1[top1 : top1 + rows1, 0:cols1] = coarse[...]
    above = slice(GUARD, top1)
    beside = slice(top1, top1 + rows1)
    below = slice(top1 + rows1, top1 + rows1 + HALO1)
    own = slice(0, cols1)
    to_right = slice(cols1, cols1 + 128)
    to_left = slice(cols1 + 128, width1)
    for ref, drow, dcol, at_rows, at_cols in (
        (up, -1, 0, above, own),
        (down, 1, 0, below, own),
        (left, 0, -1, beside, to_left),
        (right, 0, 1, beside, to_right),
        (upleft, -1, -1, above, to_left),
        (upright, -1, 1, above, to_right),
        (downleft, 1, -1, below, to_left),
        (downright, 1, 1, below, to_right),
    ):

        @pl.when(neighbour_exists(drow, dcol))
        def _():
            source1[at_rows, at_cols] = ref[...]

    inside1 = col_inside(width1, cols1, 128)
    gain1 = jnp.where(inside1, 0.8 / centre(1), 0.0)
    first_sweep(one, source1, gain1, rows1, HALO1, tiles1)
    sweep(one, two, source1, gain1, rows1, HALO1, tiles1)
    sweep(two, one, source1, gain1, rows1, HALO1, tiles1)

    def residual(tile, start):
        middle, near = neighbours(one, start)
        two[pl.ds(start + 8, 8), :] = source1[pl.ds(start + 8, 8), :] - centre(1) * middle + near

    for_tiles(0, tiles1, residual)
    count1 = 8 * tiles1
    body1 = slice(GUARD, GUARD + count1)
    rows_matrix = pair_rows(144, count1)
    pairs = pair_cols()
    source2 = jnp.concatenate(
        [
            times(apply_rows(rows_matrix, two[body1, 256 * k : 256 * k + 256]), pairs)
            for k in range(width1 // 256)
        ],
        axis=1,
    )
    e2 = coarse_levels(source2, rows1 // 2, cols1 // 2)

    spread, spread_tail = interleave(), interleave_tail()
    matrix = spread_rows(count1, 144, 0)
    even, odd = spread_cols(e2)
    mask_rows = row_inside(count1, rows1, HALO1)
    for k in range(width1 // 256):
        at = slice(256 * k, 256 * k + 256)
        total = one[body1, at] + apply_rows(matrix, times(joined(even, odd, k), spread))
        one[body1, at] = jnp.where(mask_rows & inside1[:, at], total, 0.0)
    sweep(one, two, source1, gain1, rows1, HALO1, tiles1)
    sweep(two, one, source1, gain1, rows1, HALO1, tiles1)
    sweep(one, two, source1, gain1, rows1, HALO1, tiles1)

    rows, cols = image.shape
    width = wide_noisy.shape[1]
    count = rows + 2 * HALO0
    tiles = count // 8
    body0 = slice(GUARD, GUARD + count)
    inside = col_inside(width, cols, 64)
    gain = jnp.where(inside, 0.8 / centre(0), 0.0)
    mask_rows = row_inside(count, rows, HALO0)
    near1 = two[GUARD + HALO1 - 8 : GUARD + HALO1 - 8 + 144, :]
    matrix = spread_rows(count, 144, 4)
    even, odd = spread_cols(near1)

    def add(at, wide):
        total = values[body0, at] + apply_rows(matrix, wide)
        values[body0, at] = jnp.where(mask_rows & inside[:, at], total, 0.0)

    for k in range(cols // 256):
        add(slice(256 * k, 256 * k + 256), times(joined(even, odd, k), spread))
    lane = iota((1, 128), 1)
    last = [jnp.where(lane < 64, x[:, cols1 : cols1 + 128], x[:, cols1 + 128 : width1]) for x in (even, odd)]
    add(slice(cols, width), times(jnp.concatenate(last, axis=1), spread_tail))

    sweep(values, other, source, gain, rows, HALO0, tiles)
    sweep(other, values, source, gain, rows, HALO0, tiles)

    def last_sweep(tile, start):
        middle, near = neighbours(values, start)
        k = gain * tile_valid(tile, rows, HALO0)
        s = source[pl.ds(start + 8, 8), :]
        e = 0.2 * middle + k * (s + near)
        other[pl.ds(start + 8, 8), :] = e + (wide_noisy[pl.ds(start + 8, 8), :] + 0.25 * s)

    for_tiles(0, tiles, last_sweep)

    half_cols = half_cols_mask(width, cols, 64)

    def dual_step(tile, start):
        x = other[pl.ds(start + 8, 16), :]
        w = x[0:8]
        half_rows = 0.5 * dual_masks(tile, rows, width, cols, HALO0, 64)
        here = pl.ds(start + 8, 8)
        qa = dual_a[here, :] + half_rows * (x[1:9] - w)
        qb = dual_b[here, :] + half_cols * (east(w) - w)
        a, b = shrunk(qa, qb, wide_strength[here, :])
        new_a[here, :] = a
        return w, a, b

    dual_step(0, 0)

    def last_step(tile, start):
        w, a, b = dual_step(tile, start)
        above = new_a[pl.ds(start, 16), :][7:15]
        d = (a - above) + (b - west(b))
        out = pl.ds(pl.multiple_of(start - 8, 8), 8)
        noisy = wide_noisy[pl.ds(start + 8, 8), :]
        image[out, :] = (0.8 * w + 0.2 * (d + noisy))[:, 0:cols]
        dual[0, out, :] = a[:, 0:cols]
        dual[1, out, :] = b[:, 0:cols]

    for_tiles(1, tiles - 1, last_step, unroll=1)


def in_vmem(count):
    return [pl.BlockSpec(memory_space=VMEM)] * count


def shapes(*dims):
    return [jax.ShapeDtypeStruct(d, F32) for d in dims]


def from_directions(pieces):
    up_sent, down_sent, left_sent, right_sent, ul, ur, dl, dr = pieces
    return (down_sent, up_sent, right_sent, left_sent, dr, dl, ur, ul)


def per_device(noisy, strength):
    rows, cols = noisy.shape
    sems = [pltpu.SemaphoreType.DMA((8,)), pltpu.SemaphoreType.DMA((8,))]
    pieces = pl.pallas_call(
        exchange_image,
        out_shape=shapes(*[(16, cols)] * 2, *[(32, 128)] * 2, *[(16, 128)] * 4),
        in_specs=in_vmem(2),
        out_specs=in_vmem(8),
        scratch_shapes=[VMEM((2, 16, cols), F32), VMEM((2, 32, 128), F32), VMEM((4, 16, 128), F32)] + sems,
        compiler_params=pltpu.CompilerParams(
            collective_id=0, has_side_effects=True, vmem_limit_bytes=VMEM_LIMIT
        ),
    )(noisy, strength)
    wide = (rows + 2 * HALO0 + 2 * GUARD, cols + 128)
    rows1, cols1 = rows // 2, cols // 2
    *kept, coarse = pl.pallas_call(
        down_level0,
        out_shape=shapes(*[wide] * 6, (rows1, cols1)),
        in_specs=in_vmem(10),
        out_specs=in_vmem(7),
        scratch_shapes=[VMEM(wide, F32)],
        compiler_params=pltpu.CompilerParams(vmem_limit_bytes=VMEM_LIMIT),
    )(noisy, strength, *from_directions(pieces))
    pieces = pl.pallas_call(
        exchange_source,
        out_shape=shapes(
            *[(HALO1, cols1)] * 2, *[(rows1, 128)] * 2, *[(HALO1, 128)] * 4
        ),
        in_specs=in_vmem(1),
        out_specs=in_vmem(8),
        scratch_shapes=sems,
        compiler_params=pltpu.CompilerParams(
            collective_id=1, has_side_effects=True, vmem_limit_bytes=VMEM_LIMIT
        ),
    )(coarse)
    wide1 = (rows1 + 2 * HALO1 + 2 * GUARD, cols1 + 256)
    image, dual = pl.pallas_call(
        up_levels,
        out_shape=shapes((rows, cols), (2, rows, cols)),
        in_specs=in_vmem(15),
        out_specs=in_vmem(2),
        scratch_shapes=[VMEM(wide1, F32)] * 3 + [VMEM(wide, F32)] * 2,
        input_output_aliases={},
        compiler_params=pltpu.CompilerParams(vmem_limit_bytes=VMEM_LIMIT),
    )(coarse, *from_directions(pieces), *kept)
    return image, dual


def solution(mesh):
    placed = (P("row", "col"), P("row", "col"))
    return jax.shard_map(
        per_device,
        mesh=mesh,
        in_specs=placed,
        out_specs=(P("row", "col"), P(None, "row", "col")),
        check_vma=False,
    )
```

```python
from functools import partial

import jax
import jax.numpy as jnp
from jax import lax
from jax.experimental import pallas as pl
from jax.experimental.pallas import tpu as pltpu
from jax.sharding import PartitionSpec as P

F32 = jnp.float32
BF16 = jnp.bfloat16
MESH = pl.DeviceIdType.MESH
VMEM = pltpu.VMEM

damping = 0.01
GUARD = 8
HALO0 = 8
HALO1 = 72
CHUNK = 16
DIRECTIONS = ((-1, 0), (1, 0), (0, -1), (0, 1), (-1, -1), (-1, 1), (1, -1), (1, 1))
VMEM_LIMIT = 58 * 1024 * 1024


def centre(level):
    return 4.0 + damping * 4.0**level


def iota(shape, dim):
    return lax.broadcasted_iota(jnp.int32, shape, dim)


def west(x):
    return pltpu.roll(x, 1, 1)


def east(x):
    return pltpu.roll(x, x.shape[1] - 1, 1)


def north(x):
    return pltpu.roll(x, 1, 0)


def south(x):
    return pltpu.roll(x, x.shape[0] - 1, 0)


def split(x):
    high = x.astype(BF16)
    return high, (x - high.astype(F32)).astype(BF16)


def times(x, matrix):
    high, low = split(x)
    return jnp.dot(high, matrix, preferred_element_type=F32) + jnp.dot(
        low, matrix, preferred_element_type=F32
    )


def apply_rows(matrix, x):
    high, low = split(x)
    return jnp.dot(matrix, high, preferred_element_type=F32) + jnp.dot(
        matrix, low, preferred_element_type=F32
    )


def as_matrix(mask):
    return jnp.where(mask, 1.0, 0.0).astype(BF16)


def pair_rows(coarse, fine):
    return as_matrix((iota((coarse, fine), 1) >> 1) == iota((coarse, fine), 0))


def pair_cols():
    return as_matrix((iota((256, 128), 0) >> 1) == iota((256, 128), 1))


def pair_cols_tail():
    i = iota((128, 128), 0)
    return as_matrix((i >> 1) + jnp.where(i >= 64, 64, 0) == iota((128, 128), 1))


def interleave():
    i = iota((256, 256), 0)
    return as_matrix(2 * (i & 127) + (i >> 7) == iota((256, 256), 1))


def interleave_tail():
    i = iota((256, 128), 0)
    n = iota((256, 128), 1)
    return as_matrix(2 * (i & 127) + (i >> 7) == n + jnp.where(n >= 64, 128, 0))


def spread_rows(fine, coarse, offset):
    f = iota((fine, coarse), 0)
    k = iota((fine, coarse), 1)
    near = (f >> 1) + offset
    far = near + 2 * (f & 1) - 1
    return (jnp.where(k == near, 0.75, 0.0) + jnp.where(k == far, 0.25, 0.0)).astype(BF16)


def spread_cols(c):
    return 0.75 * c + 0.25 * west(c), 0.75 * c + 0.25 * east(c)


def joined(even, odd, block):
    at = slice(128 * block, 128 * block + 128)
    return jnp.concatenate([even[:, at], odd[:, at]], axis=1)


def col_index(width, own, right):
    lane = iota((1, width), 1)
    return lax.axis_index("col") * own + jnp.where(lane < own + right, lane, lane - width)


def col_inside(width, own, right):
    g = col_index(width, own, right)
    return (g >= 0) & (g < own * lax.axis_size("col"))


def row_inside(count, own, halo):
    g = lax.axis_index("row") * own - halo + iota((count, 1), 0)
    return (g >= 0) & (g < own * lax.axis_size("row"))


def weights(level, count, width, own_rows, own_cols, halo, right):
    inside = row_inside(count, own_rows, halo) & col_inside(width, own_cols, right)
    return jnp.where(inside, 0.8 / centre(level), 0.0)


def neighbour_exists(drow, dcol):
    row = lax.axis_index("row") + drow
    col = lax.axis_index("col") + dcol
    return (
        (row >= 0) & (row < lax.axis_size("row")) & (col >= 0) & (col < lax.axis_size("col"))
    )


def exchange(sources, targets, send_sem, recv_sem):
    barrier = pltpu.get_barrier_semaphore()
    row, col = lax.axis_index("row"), lax.axis_index("col")
    for drow, dcol in DIRECTIONS:

        @pl.when(neighbour_exists(drow, dcol))
        def _():
            pl.semaphore_signal(
                barrier, inc=1, device_id=(row + drow, col + dcol), device_id_type=MESH
            )

    pl.semaphore_wait(
        barrier, sum(jnp.where(neighbour_exists(*d), 1, 0) for d in DIRECTIONS)
    )

    def copy(d):
        drow, dcol = DIRECTIONS[d]
        return pltpu.make_async_remote_copy(
            src_ref=sources[d],
            dst_ref=targets[d],
            send_sem=send_sem.at[d],
            recv_sem=recv_sem.at[d],
            device_id=(row + drow, col + dcol),
            device_id_type=MESH,
        )

    order = (2, 3, 4, 5, 6, 7, 0, 1)
    for d in order:

        @pl.when(neighbour_exists(*DIRECTIONS[d]))
        def _():
            copy(d).start()

    for d in order:
        drow, dcol = DIRECTIONS[d]

        @pl.when(neighbour_exists(drow, dcol))
        def _():
            copy(d).wait_send()

        @pl.when(neighbour_exists(-drow, -dcol))
        def _():
            copy(d).wait_recv()


def exchange_image(
    noisy, strength, *rest
):
    targets, scratch = rest[:8], rest[8:]
    vertical, sides, corners, send_sem, recv_sem = scratch
    rows, cols = noisy.shape
    lane = iota((16, 128), 1)
    for k, ref in enumerate((noisy, strength)):
        at = slice(8 * k, 8 * k + 8)
        vertical[0, at] = ref[0:8, :]
        vertical[1, at] = ref[rows - 8 : rows, :]
        corners[0, at] = ref[0:8, 0:128]
        corners[1, at] = ref[0:8, cols - 128 : cols]
        corners[2, at] = ref[rows - 8 : rows, 0:128]
        corners[3, at] = ref[rows - 8 : rows, cols - 128 : cols]
        first = jnp.zeros((16, 128), F32)
        last = jnp.zeros((16, 128), F32)
        for g in range(16):
            here = (lane >= 8 * g) & (lane < 8 * g + 8)
            near = slice(16 * g, 16 * g + 16)
            first = jnp.where(here, pltpu.roll(ref[near, 0:128], 8 * g, 1), first)
            last = jnp.where(
                here, pltpu.roll(ref[near, cols - 128 : cols], (8 * g + 8) % 128, 1), last
            )
        sides[0, 16 * k : 16 * k + 16] = first
        sides[1, 16 * k : 16 * k + 16] = last
    sources = (
        vertical.at[0],
        vertical.at[1],
        sides.at[0],
        sides.at[1],
        corners.at[0],
        corners.at[1],
        corners.at[2],
        corners.at[3],
    )
    exchange(sources, targets, send_sem, recv_sem)


def exchange_source(source, *rest):
    targets, (send_sem, recv_sem) = rest[:8], rest[8:]
    rows, cols = source.shape
    up, down = pl.ds(0, HALO1), pl.ds(rows - HALO1, HALO1)
    left, right = pl.ds(0, 128), pl.ds(cols - 128, 128)
    sources = (
        source.at[up, :],
        source.at[down, :],
        source.at[:, left],
        source.at[:, right],
        source.at[up, left],
        source.at[up, right],
        source.at[down, left],
        source.at[down, right],
    )
    exchange(sources, targets, send_sem, recv_sem)


def tile_valid(tile, own, halo):
    g = lax.axis_index("row") * own - halo + tile * 8
    return jnp.where((g >= 0) & (g < own * lax.axis_size("row")), 1.0, 0.0)


def chunk_gain(gain, tile, own, halo):
    wide = jnp.broadcast_to(gain, (8, gain.shape[1]))
    return jnp.concatenate(
        [wide * tile_valid(tile + k, own, halo) for k in range(CHUNK // 8)], axis=0
    )


def neighbours(ref, start):
    x = ref[pl.ds(start, CHUNK + 16), :]
    middle = x[8 : CHUNK + 8]
    return middle, (x[7 : CHUNK + 7] + x[9 : CHUNK + 9]) + (west(middle) + east(middle))


def for_chunks(first, tiles, body, unroll=1):
    def step(chunk, carry):
        tile = first + chunk * (CHUNK // 8)
        body(tile, pl.multiple_of(tile * 8, 8))
        return carry

    lax.fori_loop(0, tiles * 8 // CHUNK, step, 0, unroll=unroll)


def inner(start):
    return pl.ds(start + 8, CHUNK)


def sweep(old, new, source, gain, own, halo, first, tiles):
    def body(tile, start):
        middle, beside = neighbours(old, start)
        k = chunk_gain(gain, tile, own, halo)
        new[inner(start), :] = 0.2 * middle + k * (source[inner(start), :] + beside)

    for_chunks(first, tiles, body)


def first_sweep(new, source, gain, own, halo, tiles):
    def body(tile, start):
        k = chunk_gain(gain, tile, own, halo)
        new[inner(start), :] = k * source[inner(start), :]

    for_chunks(0, tiles, body)


def dual_masks(tile, count, own_rows, halo):
    g = lax.axis_index("row") * own_rows - halo + tile * 8 + iota((count, 1), 0)
    return jnp.where((g >= 0) & (g < own_rows * lax.axis_size("row") - 1), 1.0, 0.0)


def shrunk(qa, qb, bound):
    shrink = jnp.minimum(1.0, bound * lax.rsqrt(qa * qa + qb * qb))
    return qa * shrink, qb * shrink


def clear_guards(ref):
    rows, width = ref.shape
    ref[0:GUARD, :] = jnp.zeros((GUARD, width), ref.dtype)
    ref[rows - GUARD : rows, :] = jnp.zeros((GUARD, width), ref.dtype)


def half_cols_mask(width, own, right):
    g = col_index(width, own, right)
    return jnp.where((g >= 0) & (g < own * lax.axis_size("col") - 1), 0.5, 0.0)


def down_level0(
    noisy, strength, up, down, left, right, upleft, upright, downleft, downright,
    wide_noisy, wide_strength, dual_a, dual_b, source, values, coarse, other,
):
    rows, cols = noisy.shape
    width = wide_noisy.shape[1]
    total = wide_noisy.shape[0]
    tiles = (total - 2 * GUARD) // 8
    lane = iota((16, 128), 1)
    right_end = jnp.where(neighbour_exists(0, 1), 8, 0)
    left_start = jnp.where(neighbour_exists(0, -1), 120, 128)
    top = GUARD + HALO0
    for k, (ref, wide, fill) in enumerate(((noisy, wide_noisy, 0.0), (strength, wide_strength, 1.0))):
        wide[top : top + rows, 0:cols] = ref[...]
        wide[0:top, :] = jnp.full((top, width), fill, F32)
        wide[top + rows : total, :] = jnp.full((total - top - rows, width), fill, F32)
        from_right = right[16 * k : 16 * k + 16]
        from_left = left[16 * k : 16 * k + 16]
        for g in range(16):
            piece = jnp.where(
                lane < right_end,
                pltpu.roll(from_right, (128 - 8 * g) % 128, 1),
                jnp.where(lane >= left_start, pltpu.roll(from_left, (120 - 8 * g) % 128, 1), fill),
            )
            wide[top + 16 * g : top + 16 * g + 16, cols:width] = piece
        at = slice(8 * k, 8 * k + 8)
        lane8 = lane[0:8]
        for edge, other_left, other_right, drow, place in (
            (up, upleft, upright, -1, GUARD),
            (down, downleft, downright, 1, top + rows),
        ):

            @pl.when(neighbour_exists(drow, 0))
            def _():
                wide[place : place + 8, 0:cols] = edge[at, :]
                wide[place : place + 8, cols:width] = jnp.where(
                    lane8 < right_end,
                    other_right[at, :],
                    jnp.where(lane8 >= left_start, other_left[at, :], fill),
                )

    for ref in (dual_a, dual_b, source, values, other):
        clear_guards(ref)

    inside = col_inside(width, cols, 64)
    gain = jnp.where(inside, 0.8 / centre(0), 0.0)
    half_cols = half_cols_mask(width, cols, 64)

    def first_step(tile, start):
        x = wide_noisy[pl.ds(start + 8, CHUNK + 8), :]
        w = x[0:CHUNK]
        half_rows = 0.5 * dual_masks(tile, CHUNK, rows, HALO0)
        qa = half_rows * (x[1 : CHUNK + 1] - w)
        qb = half_cols * (east(w) - w)
        before = dual_a[pl.ds(start, 8), :]
        a, b = shrunk(qa, qb, wide_strength[inner(start), :])
        dual_a[inner(start), :] = a
        dual_b[inner(start), :] = b
        above = jnp.concatenate([before, a], axis=0)[7 : CHUNK + 7]
        s = 0.8 * ((a - above) + (b - west(b)))
        source[inner(start), :] = s
        values[inner(start), :] = chunk_gain(gain, tile, rows, HALO0) * s

    for_chunks(0, tiles, first_step)
    sweep(values, other, source, gain, rows, HALO0, 0, tiles)
    sweep(other, values, source, gain, rows, HALO0, 0, tiles)

    def residual(tile, start):
        middle, beside = neighbours(values, start)
        other[inner(start), :] = source[inner(start), :] - centre(0) * middle + beside

    for_chunks(1, tiles - 2, residual)
    rows_matrix = pair_rows(rows // 2, rows)
    cols_matrix = pair_cols()
    for block in range(cols // 256):
        piece = other[top : top + rows, 256 * block : 256 * block + 256]
        coarse[:, 128 * block : 128 * block + 128] = times(
            apply_rows(rows_matrix, piece), cols_matrix
        )


def relax(e, source, gain):
    beside = (north(e) + south(e)) + (west(e) + east(e))
    return 0.2 * e + gain * (source + beside)


def smoothed(source, gain):
    e = gain * source
    e = relax(e, source, gain)
    return relax(e, source, gain)


def remaining(e, source, level):
    return source - centre(level) * e + ((north(e) + south(e)) + (west(e) + east(e)))


def coarse_levels(source2, own_rows, own_cols):
    n2, n3, n4 = 144, 80, 48
    gain2 = weights(2, n2, own_cols + 128, own_rows, own_cols, 36, 64)
    gain3 = weights(3, n3, 256, own_rows // 2, own_cols // 2, 18, 64)
    gain4 = weights(4, n4, 128, own_rows // 4, own_cols // 4, 9, 32)
    spread, spread_tail = interleave(), interleave_tail()
    pairs, pairs_tail = pair_cols(), pair_cols_tail()

    e2 = smoothed(source2, gain2)
    left = apply_rows(pair_rows(n3, n2), remaining(e2, source2, 2))
    source3 = jnp.concatenate(
        [times(left[:, 0:256], pairs), times(left[:, 256:384], pairs_tail)], axis=1
    )
    e3 = smoothed(source3, gain3)
    source4 = times(apply_rows(pair_rows(n4, n3), remaining(e3, source3, 3)), pairs)
    e4 = smoothed(source4, gain4)

    even, odd = spread_cols(e4)
    wide = times(joined(even, odd, 0), spread)
    e3 = e3 + apply_rows(spread_rows(n3, n4, 0), wide)
    e3 = jnp.where(gain3 > 0.0, e3, 0.0)
    for _ in range(3):
        e3 = relax(e3, source3, gain3)

    even, odd = spread_cols(e3)
    wide = jnp.concatenate(
        [times(joined(even, odd, 0), spread), times(joined(even, odd, 1), spread_tail)], axis=1
    )
    kept = slice(24, 120)
    e2, source2, gain2 = e2[kept], source2[kept], gain2[kept]
    e2 = e2 + apply_rows(spread_rows(96, n3, 12), wide)
    e2 = jnp.where(gain2 > 0.0, e2, 0.0)
    for _ in range(3):
        e2 = relax(e2, source2, gain2)
    return e2


def up_levels(
    coarse, up, down, left, right, upleft, upright, downleft, downright,
    *rest,
):
    far, (image, dual), local = rest[:6], rest[6:8], rest[8:14]
    source1, one, two, other, new_a, fetched = rest[14:]
    wide_noisy, wide_strength, dual_a, dual_b, source, values = local
    copies = [
        pltpu.make_async_copy(far[k], local[k], fetched.at[k]) for k in range(len(far))
    ]
    for copy in copies:
        copy.start()
    rows1, cols1 = coarse.shape
    width1 = cols1 + 256
    tiles1 = (source1.shape[0] - 2 * GUARD) // 8
    top1 = GUARD + HALO1
    source1[...] = jnp.zeros(source1.shape, F32)
    for ref in (one, two, other, new_a):
        clear_guards(ref)
    source1[top1 : top1 + rows1, 0:cols1] = coarse[...]
    above = slice(GUARD, top1)
    beside = slice(top1, top1 + rows1)
    below = slice(top1 + rows1, top1 + rows1 + HALO1)
    own = slice(0, cols1)
    to_right = slice(cols1, cols1 + 128)
    to_left = slice(cols1 + 128, width1)
    for ref, drow, dcol, at_rows, at_cols in (
        (up, -1, 0, above, own),
        (down, 1, 0, below, own),
        (left, 0, -1, beside, to_left),
        (right, 0, 1, beside, to_right),
        (upleft, -1, -1, above, to_left),
        (upright, -1, 1, above, to_right),
        (downleft, 1, -1, below, to_left),
        (downright, 1, 1, below, to_right),
    ):

        @pl.when(neighbour_exists(drow, dcol))
        def _():
            source1[at_rows, at_cols] = ref[...]

    inside1 = col_inside(width1, cols1, 128)
    gain1 = jnp.where(inside1, 0.8 / centre(1), 0.0)
    first_sweep(one, source1, gain1, rows1, HALO1, tiles1)
    sweep(one, two, source1, gain1, rows1, HALO1, 0, tiles1)
    sweep(two, one, source1, gain1, rows1, HALO1, 0, tiles1)

    def residual(tile, start):
        middle, near = neighbours(one, start)
        two[inner(start), :] = source1[inner(start), :] - centre(1) * middle + near

    for_chunks(0, tiles1, residual)
    count1 = 8 * tiles1
    body1 = slice(GUARD, GUARD + count1)
    rows_matrix = pair_rows(144, count1)
    pairs = pair_cols()
    source2 = jnp.concatenate(
        [
            times(apply_rows(rows_matrix, two[body1, 256 * k : 256 * k + 256]), pairs)
            for k in range(width1 // 256)
        ],
        axis=1,
    )
    e2 = coarse_levels(source2, rows1 // 2, cols1 // 2)

    spread, spread_tail = interleave(), interleave_tail()
    near_first = (HALO1 - 8) // 8
    near_count = rows1 + 16
    near_rows = slice(GUARD + HALO1 - 8, GUARD + HALO1 - 8 + near_count)
    matrix = spread_rows(near_count, 96, 8)
    even, odd = spread_cols(e2)
    mask_rows = row_inside(near_count, rows1, 8)
    for k in range(width1 // 256):
        at = slice(256 * k, 256 * k + 256)
        total = one[near_rows, at] + apply_rows(matrix, times(joined(even, odd, k), spread))
        one[near_rows, at] = jnp.where(mask_rows & inside1[:, at], total, 0.0)
    sweep(one, two, source1, gain1, rows1, HALO1, near_first, near_count // 8)
    sweep(two, one, source1, gain1, rows1, HALO1, near_first, near_count // 8)
    sweep(one, two, source1, gain1, rows1, HALO1, near_first, near_count // 8)

    for copy in copies:
        copy.wait()
    rows, cols = image.shape
    width = wide_noisy.shape[1]
    count = rows + 2 * HALO0
    tiles = count // 8
    body0 = slice(GUARD, GUARD + count)
    inside = col_inside(width, cols, 64)
    gain = jnp.where(inside, 0.8 / centre(0), 0.0)
    mask_rows = row_inside(count, rows, HALO0)
    near1 = two[near_rows, :]
    matrix = spread_rows(count, near_count, 4)
    even, odd = spread_cols(near1)

    def add(at, wide):
        total = values[body0, at] + apply_rows(matrix, wide)
        values[body0, at] = jnp.where(mask_rows & inside[:, at], total, 0.0)

    for k in range(cols // 256):
        add(slice(256 * k, 256 * k + 256), times(joined(even, odd, k), spread))
    lane = iota((1, 128), 1)
    last = [jnp.where(lane < 64, x[:, cols1 : cols1 + 128], x[:, cols1 + 128 : width1]) for x in (even, odd)]
    add(slice(cols, width), times(jnp.concatenate(last, axis=1), spread_tail))

    sweep(values, other, source, gain, rows, HALO0, 0, tiles)
    sweep(other, values, source, gain, rows, HALO0, 0, tiles)

    def last_sweep(tile, start):
        middle, near = neighbours(values, start)
        k = chunk_gain(gain, tile, rows, HALO0)
        s = source[inner(start), :]
        e = 0.2 * middle + k * (s + near)
        other[inner(start), :] = e + (wide_noisy[inner(start), :] + 0.25 * s)

    for_chunks(0, tiles, last_sweep)

    half_cols = half_cols_mask(width, cols, 64)

    def dual_step(tile, start, size):
        x = other[pl.ds(start + 8, size + 8), :]
        w = x[0:size]
        half_rows = 0.5 * dual_masks(tile, size, rows, HALO0)
        here = pl.ds(start + 8, size)
        qa = dual_a[here, :] + half_rows * (x[1 : size + 1] - w)
        qb = dual_b[here, :] + half_cols * (east(w) - w)
        a, b = shrunk(qa, qb, wide_strength[here, :])
        return w, a, b

    new_a[8:16, :] = dual_step(0, 0, 8)[1]

    def last_step(tile, start):
        before = new_a[pl.ds(start, 8), :]
        w, a, b = dual_step(tile, start, CHUNK)
        new_a[inner(start), :] = a
        above = jnp.concatenate([before, a], axis=0)[7 : CHUNK + 7]
        d = (a - above) + (b - west(b))
        out = pl.ds(pl.multiple_of(start - 8, 8), CHUNK)
        noisy = wide_noisy[inner(start), :]
        image[out, :] = (0.8 * w + 0.2 * (d + noisy))[:, 0:cols]
        dual[0, out, :] = a[:, 0:cols]
        dual[1, out, :] = b[:, 0:cols]

    for_chunks(1, tiles - 2, last_step)


def in_vmem(count):
    return [pl.BlockSpec(memory_space=VMEM)] * count


def shapes(*dims):
    return [jax.ShapeDtypeStruct(d, F32) for d in dims]


def from_directions(pieces):
    up_sent, down_sent, left_sent, right_sent, ul, ur, dl, dr = pieces
    return (down_sent, up_sent, right_sent, left_sent, dr, dl, ur, ul)


def per_device(noisy, strength):
    rows, cols = noisy.shape
    sems = [pltpu.SemaphoreType.DMA((8,)), pltpu.SemaphoreType.DMA((8,))]
    pieces = pl.pallas_call(
        exchange_image,
        out_shape=shapes(*[(16, cols)] * 2, *[(32, 128)] * 2, *[(16, 128)] * 4),
        in_specs=in_vmem(2),
        out_specs=in_vmem(8),
        scratch_shapes=[VMEM((2, 16, cols), F32), VMEM((2, 32, 128), F32), VMEM((4, 16, 128), F32)] + sems,
        compiler_params=pltpu.CompilerParams(
            collective_id=0, has_side_effects=True, vmem_limit_bytes=VMEM_LIMIT
        ),
    )(noisy, strength)
    wide = (rows + 2 * HALO0 + 2 * GUARD, cols + 128)
    rows1, cols1 = rows // 2, cols // 2
    *kept, coarse = pl.pallas_call(
        down_level0,
        out_shape=shapes(*[wide] * 6, (rows1, cols1)),
        in_specs=in_vmem(10),
        out_specs=in_vmem(7),
        scratch_shapes=[VMEM(wide, F32)],
        compiler_params=pltpu.CompilerParams(vmem_limit_bytes=VMEM_LIMIT),
    )(noisy, strength, *from_directions(pieces))
    pieces = pl.pallas_call(
        exchange_source,
        out_shape=shapes(
            *[(HALO1, cols1)] * 2, *[(rows1, 128)] * 2, *[(HALO1, 128)] * 4
        ),
        in_specs=in_vmem(1),
        out_specs=in_vmem(8),
        scratch_shapes=sems,
        compiler_params=pltpu.CompilerParams(
            collective_id=1, has_side_effects=True, vmem_limit_bytes=VMEM_LIMIT
        ),
    )(coarse)
    wide1 = (rows1 + 2 * HALO1 + 2 * GUARD, cols1 + 256)
    image, dual = pl.pallas_call(
        up_levels,
        out_shape=shapes((rows, cols), (2, rows, cols)),
        in_specs=in_vmem(9) + [pl.BlockSpec(memory_space=pl.ANY)] * 6,
        out_specs=in_vmem(2),
        scratch_shapes=[VMEM(wide, F32)] * 6
        + [VMEM(wide1, F32)] * 3
        + [VMEM(wide, F32)] * 2
        + [pltpu.SemaphoreType.DMA((6,))],
        compiler_params=pltpu.CompilerParams(vmem_limit_bytes=VMEM_LIMIT),
    )(coarse, *from_directions(pieces), *kept)
    return image, dual


def solution(mesh):
    placed = (P("row", "col"), P("row", "col"))
    return jax.shard_map(
        per_device,
        mesh=mesh,
        in_specs=placed,
        out_specs=(P("row", "col"), P(None, "row", "col")),
        check_vma=False,
    )
```

```python
from functools import partial

import jax
import jax.numpy as jnp
from jax import lax
from jax.experimental import pallas as pl
from jax.experimental.pallas import tpu as pltpu
from jax.sharding import PartitionSpec as P

F32 = jnp.float32
BF16 = jnp.bfloat16
MESH = pl.DeviceIdType.MESH
VMEM = pltpu.VMEM

damping = 0.01
GUARD = 8
HALO0 = 8
HALO1 = 72
CHUNK = 16
DIRECTIONS = ((-1, 0), (1, 0), (0, -1), (0, 1), (-1, -1), (-1, 1), (1, -1), (1, 1))
VMEM_LIMIT = 58 * 1024 * 1024


def centre(level):
    return 4.0 + damping * 4.0**level


def iota(shape, dim):
    return lax.broadcasted_iota(jnp.int32, shape, dim)


def west(x):
    return pltpu.roll(x, 1, 1)


def east(x):
    return pltpu.roll(x, x.shape[1] - 1, 1)


def north(x):
    return pltpu.roll(x, 1, 0)


def south(x):
    return pltpu.roll(x, x.shape[0] - 1, 0)


def split(x):
    high = x.astype(BF16)
    return high, (x - high.astype(F32)).astype(BF16)


def times(x, matrix):
    high, low = split(x)
    return jnp.dot(high, matrix, preferred_element_type=F32) + jnp.dot(
        low, matrix, preferred_element_type=F32
    )


def apply_rows(matrix, x):
    high, low = split(x)
    return jnp.dot(matrix, high, preferred_element_type=F32) + jnp.dot(
        matrix, low, preferred_element_type=F32
    )


def as_matrix(mask):
    return jnp.where(mask, 1.0, 0.0).astype(BF16)


def pair_rows(coarse, fine):
    return as_matrix((iota((coarse, fine), 1) >> 1) == iota((coarse, fine), 0))


def pair_cols():
    return as_matrix((iota((256, 128), 0) >> 1) == iota((256, 128), 1))


def pair_cols_tail():
    i = iota((128, 128), 0)
    return as_matrix((i >> 1) + jnp.where(i >= 64, 64, 0) == iota((128, 128), 1))


def interleave():
    i = iota((256, 256), 0)
    return as_matrix(2 * (i & 127) + (i >> 7) == iota((256, 256), 1))


def interleave_tail():
    i = iota((256, 128), 0)
    n = iota((256, 128), 1)
    return as_matrix(2 * (i & 127) + (i >> 7) == n + jnp.where(n >= 64, 128, 0))


def spread_rows(fine, coarse, offset):
    f = iota((fine, coarse), 0)
    k = iota((fine, coarse), 1)
    near = (f >> 1) + offset
    far = near + 2 * (f & 1) - 1
    return (jnp.where(k == near, 0.75, 0.0) + jnp.where(k == far, 0.25, 0.0)).astype(BF16)


def spread_cols(c):
    return 0.75 * c + 0.25 * west(c), 0.75 * c + 0.25 * east(c)


def joined(even, odd, block):
    at = slice(128 * block, 128 * block + 128)
    return jnp.concatenate([even[:, at], odd[:, at]], axis=1)


def col_index(width, own, right):
    lane = iota((1, width), 1)
    return lax.axis_index("col") * own + jnp.where(lane < own + right, lane, lane - width)


def col_inside(width, own, right):
    g = col_index(width, own, right)
    return (g >= 0) & (g < own * lax.axis_size("col"))


def row_inside(count, own, halo):
    g = lax.axis_index("row") * own - halo + iota((count, 1), 0)
    return (g >= 0) & (g < own * lax.axis_size("row"))


def weights(level, count, width, own_rows, own_cols, halo, right):
    inside = row_inside(count, own_rows, halo) & col_inside(width, own_cols, right)
    return jnp.where(inside, 0.8 / centre(level), 0.0)


def neighbour_exists(drow, dcol):
    row = lax.axis_index("row") + drow
    col = lax.axis_index("col") + dcol
    return (
        (row >= 0) & (row < lax.axis_size("row")) & (col >= 0) & (col < lax.axis_size("col"))
    )


def exchange(sources, targets, send_sem, recv_sem):
    barrier = pltpu.get_barrier_semaphore()
    row, col = lax.axis_index("row"), lax.axis_index("col")
    for drow, dcol in DIRECTIONS:

        @pl.when(neighbour_exists(drow, dcol))
        def _():
            pl.semaphore_signal(
                barrier, inc=1, device_id=(row + drow, col + dcol), device_id_type=MESH
            )

    pl.semaphore_wait(
        barrier, sum(jnp.where(neighbour_exists(*d), 1, 0) for d in DIRECTIONS)
    )

    def copy(d):
        drow, dcol = DIRECTIONS[d]
        return pltpu.make_async_remote_copy(
            src_ref=sources[d],
            dst_ref=targets[d],
            send_sem=send_sem.at[d],
            recv_sem=recv_sem.at[d],
            device_id=(row + drow, col + dcol),
            device_id_type=MESH,
        )

    order = (2, 3, 4, 5, 6, 7, 0, 1)
    for d in order:

        @pl.when(neighbour_exists(*DIRECTIONS[d]))
        def _():
            copy(d).start()

    for d in order:
        drow, dcol = DIRECTIONS[d]

        @pl.when(neighbour_exists(drow, dcol))
        def _():
            copy(d).wait_send()

        @pl.when(neighbour_exists(-drow, -dcol))
        def _():
            copy(d).wait_recv()


def exchange_image(
    noisy, strength, *rest
):
    targets, scratch = rest[:8], rest[8:]
    vertical, sides, corners, send_sem, recv_sem = scratch
    rows, cols = noisy.shape
    lane = iota((16, 128), 1)
    for k, ref in enumerate((noisy, strength)):
        at = slice(8 * k, 8 * k + 8)
        vertical[0, at] = ref[0:8, :]
        vertical[1, at] = ref[rows - 8 : rows, :]
        corners[0, at] = ref[0:8, 0:128]
        corners[1, at] = ref[0:8, cols - 128 : cols]
        corners[2, at] = ref[rows - 8 : rows, 0:128]
        corners[3, at] = ref[rows - 8 : rows, cols - 128 : cols]
        first = jnp.zeros((16, 128), F32)
        last = jnp.zeros((16, 128), F32)
        for g in range(16):
            here = (lane >= 8 * g) & (lane < 8 * g + 8)
            near = slice(16 * g, 16 * g + 16)
            first = jnp.where(here, pltpu.roll(ref[near, 0:128], 8 * g, 1), first)
            last = jnp.where(
                here, pltpu.roll(ref[near, cols - 128 : cols], (8 * g + 8) % 128, 1), last
            )
        sides[0, 16 * k : 16 * k + 16] = first
        sides[1, 16 * k : 16 * k + 16] = last
    sources = (
        vertical.at[0],
        vertical.at[1],
        sides.at[0],
        sides.at[1],
        corners.at[0],
        corners.at[1],
        corners.at[2],
        corners.at[3],
    )
    exchange(sources, targets, send_sem, recv_sem)


def exchange_source(source, *rest):
    targets, (send_sem, recv_sem) = rest[:8], rest[8:]
    rows, cols = source.shape
    up, down = pl.ds(0, HALO1), pl.ds(rows - HALO1, HALO1)
    left, right = pl.ds(0, 128), pl.ds(cols - 128, 128)
    sources = (
        source.at[up, :],
        source.at[down, :],
        source.at[:, left],
        source.at[:, right],
        source.at[up, left],
        source.at[up, right],
        source.at[down, left],
        source.at[down, right],
    )
    exchange(sources, targets, send_sem, recv_sem)


def tile_valid(tile, own, halo):
    g = lax.axis_index("row") * own - halo + tile * 8
    return jnp.where((g >= 0) & (g < own * lax.axis_size("row")), 1.0, 0.0)


def chunk_gain(gain, tile, own, halo):
    wide = jnp.broadcast_to(gain, (8, gain.shape[1]))
    return jnp.concatenate(
        [wide * tile_valid(tile + k, own, halo) for k in range(CHUNK // 8)], axis=0
    )


def neighbours(ref, start):
    x = ref[pl.ds(start, CHUNK + 16), :]
    middle = x[8 : CHUNK + 8]
    return middle, (x[7 : CHUNK + 7] + x[9 : CHUNK + 9]) + (west(middle) + east(middle))


def for_chunks(first, tiles, body, unroll=2):
    def step(chunk, carry):
        tile = first + chunk * (CHUNK // 8)
        body(tile, pl.multiple_of(tile * 8, 8))
        return carry

    lax.fori_loop(0, tiles * 8 // CHUNK, step, 0, unroll=unroll)


def inner(start):
    return pl.ds(start + 8, CHUNK)


def sweep(old, new, source, gain, own, halo, first, tiles):
    def body(tile, start):
        middle, beside = neighbours(old, start)
        k = chunk_gain(gain, tile, own, halo)
        new[inner(start), :] = 0.2 * middle + k * (source[inner(start), :] + beside)

    for_chunks(first, tiles, body)


def first_sweep(new, source, gain, own, halo, tiles):
    def body(tile, start):
        k = chunk_gain(gain, tile, own, halo)
        new[inner(start), :] = k * source[inner(start), :]

    for_chunks(0, tiles, body)


def dual_masks(tile, count, own_rows, halo):
    g = lax.axis_index("row") * own_rows - halo + tile * 8 + iota((count, 1), 0)
    return jnp.where((g >= 0) & (g < own_rows * lax.axis_size("row") - 1), 1.0, 0.0)


def shrunk(qa, qb, bound):
    shrink = jnp.minimum(1.0, bound * lax.rsqrt(qa * qa + qb * qb))
    return qa * shrink, qb * shrink


def clear_guards(ref):
    rows, width = ref.shape
    ref[0:GUARD, :] = jnp.zeros((GUARD, width), ref.dtype)
    ref[rows - GUARD : rows, :] = jnp.zeros((GUARD, width), ref.dtype)


def half_cols_mask(width, own, right):
    g = col_index(width, own, right)
    return jnp.where((g >= 0) & (g < own * lax.axis_size("col") - 1), 0.5, 0.0)


def down_level0(
    noisy, strength, up, down, left, right, upleft, upright, downleft, downright,
    *rest,
):
    far, coarse, local, (other, written) = rest[:6], rest[6], rest[7:13], rest[13:]
    wide_noisy, wide_strength, dual_a, dual_b, source, values = local
    copies = [
        pltpu.make_async_copy(local[k], far[k], written.at[k]) for k in range(len(far))
    ]
    rows, cols = noisy.shape
    width = wide_noisy.shape[1]
    total = wide_noisy.shape[0]
    tiles = (total - 2 * GUARD) // 8
    lane = iota((16, 128), 1)
    right_end = jnp.where(neighbour_exists(0, 1), 8, 0)
    left_start = jnp.where(neighbour_exists(0, -1), 120, 128)
    top = GUARD + HALO0
    for k, (ref, wide, fill) in enumerate(((noisy, wide_noisy, 0.0), (strength, wide_strength, 1.0))):
        wide[top : top + rows, 0:cols] = ref[...]
        wide[0:top, :] = jnp.full((top, width), fill, F32)
        wide[top + rows : total, :] = jnp.full((total - top - rows, width), fill, F32)
        from_right = right[16 * k : 16 * k + 16]
        from_left = left[16 * k : 16 * k + 16]
        for g in range(16):
            piece = jnp.where(
                lane < right_end,
                pltpu.roll(from_right, (128 - 8 * g) % 128, 1),
                jnp.where(lane >= left_start, pltpu.roll(from_left, (120 - 8 * g) % 128, 1), fill),
            )
            wide[top + 16 * g : top + 16 * g + 16, cols:width] = piece
        at = slice(8 * k, 8 * k + 8)
        lane8 = lane[0:8]
        for edge, other_left, other_right, drow, place in (
            (up, upleft, upright, -1, GUARD),
            (down, downleft, downright, 1, top + rows),
        ):

            @pl.when(neighbour_exists(drow, 0))
            def _():
                wide[place : place + 8, 0:cols] = edge[at, :]
                wide[place : place + 8, cols:width] = jnp.where(
                    lane8 < right_end,
                    other_right[at, :],
                    jnp.where(lane8 >= left_start, other_left[at, :], fill),
                )

    for ref in (dual_a, dual_b, source, values, other):
        clear_guards(ref)

    inside = col_inside(width, cols, 64)
    gain = jnp.where(inside, 0.8 / centre(0), 0.0)
    half_cols = half_cols_mask(width, cols, 64)

    def first_step(tile, start):
        x = wide_noisy[pl.ds(start + 8, CHUNK + 8), :]
        w = x[0:CHUNK]
        half_rows = 0.5 * dual_masks(tile, CHUNK, rows, HALO0)
        qa = half_rows * (x[1 : CHUNK + 1] - w)
        qb = half_cols * (east(w) - w)
        before = dual_a[pl.ds(start, 8), :]
        a, b = shrunk(qa, qb, wide_strength[inner(start), :])
        dual_a[inner(start), :] = a
        dual_b[inner(start), :] = b
        above = jnp.concatenate([before, a], axis=0)[7 : CHUNK + 7]
        s = 0.8 * ((a - above) + (b - west(b)))
        source[inner(start), :] = s
        values[inner(start), :] = chunk_gain(gain, tile, rows, HALO0) * s

    copies[0].start()
    copies[1].start()
    for_chunks(0, tiles, first_step)
    for copy in copies[2:5]:
        copy.start()
    sweep(values, other, source, gain, rows, HALO0, 0, tiles)
    sweep(other, values, source, gain, rows, HALO0, 0, tiles)

    copies[5].start()

    def residual(tile, start):
        middle, beside = neighbours(values, start)
        other[inner(start), :] = source[inner(start), :] - centre(0) * middle + beside

    for_chunks(1, tiles - 2, residual)
    rows_matrix = pair_rows(rows // 2, rows)
    cols_matrix = pair_cols()
    for block in range(cols // 256):
        piece = other[top : top + rows, 256 * block : 256 * block + 256]
        coarse[:, 128 * block : 128 * block + 128] = times(
            apply_rows(rows_matrix, piece), cols_matrix
        )
    for copy in copies:
        copy.wait()


def relax(e, source, gain):
    beside = (north(e) + south(e)) + (west(e) + east(e))
    return 0.2 * e + gain * (source + beside)


def smoothed(source, gain):
    e = gain * source
    e = relax(e, source, gain)
    return relax(e, source, gain)


def remaining(e, source, level):
    return source - centre(level) * e + ((north(e) + south(e)) + (west(e) + east(e)))


def coarse_levels(source2, own_rows, own_cols):
    n2, n3, n4 = 144, 80, 48
    gain2 = weights(2, n2, own_cols + 128, own_rows, own_cols, 36, 64)
    gain3 = weights(3, n3, 256, own_rows // 2, own_cols // 2, 18, 64)
    gain4 = weights(4, n4, 128, own_rows // 4, own_cols // 4, 9, 32)
    spread, spread_tail = interleave(), interleave_tail()
    pairs, pairs_tail = pair_cols(), pair_cols_tail()

    e2 = smoothed(source2, gain2)
    left = apply_rows(pair_rows(n3, n2), remaining(e2, source2, 2))
    source3 = jnp.concatenate(
        [times(left[:, 0:256], pairs), times(left[:, 256:384], pairs_tail)], axis=1
    )
    e3 = smoothed(source3, gain3)
    source4 = times(apply_rows(pair_rows(n4, n3), remaining(e3, source3, 3)), pairs)
    e4 = smoothed(source4, gain4)

    even, odd = spread_cols(e4)
    wide = times(joined(even, odd, 0), spread)
    e3 = e3 + apply_rows(spread_rows(n3, n4, 0), wide)
    e3 = jnp.where(gain3 > 0.0, e3, 0.0)
    for _ in range(3):
        e3 = relax(e3, source3, gain3)

    even, odd = spread_cols(e3)
    wide = jnp.concatenate(
        [times(joined(even, odd, 0), spread), times(joined(even, odd, 1), spread_tail)], axis=1
    )
    kept = slice(24, 120)
    e2, source2, gain2 = e2[kept], source2[kept], gain2[kept]
    e2 = e2 + apply_rows(spread_rows(96, n3, 12), wide)
    e2 = jnp.where(gain2 > 0.0, e2, 0.0)
    for _ in range(3):
        e2 = relax(e2, source2, gain2)
    return e2


def up_levels(
    coarse, up, down, left, right, upleft, upright, downleft, downright,
    *rest,
):
    far, (image_out, dual_out), local = rest[:6], rest[6:8], rest[8:14]
    source1, one, two, other, new_a, image, dual, fetched, written = rest[14:]
    wide_noisy, wide_strength, dual_a, dual_b, source, values = local
    copies = [
        pltpu.make_async_copy(far[k], local[k], fetched.at[k]) for k in range(len(far))
    ]
    for copy in copies:
        copy.start()
    rows1, cols1 = coarse.shape
    width1 = cols1 + 256
    tiles1 = (source1.shape[0] - 2 * GUARD) // 8
    top1 = GUARD + HALO1
    source1[...] = jnp.zeros(source1.shape, F32)
    for ref in (one, two, other, new_a):
        clear_guards(ref)
    source1[top1 : top1 + rows1, 0:cols1] = coarse[...]
    above = slice(GUARD, top1)
    beside = slice(top1, top1 + rows1)
    below = slice(top1 + rows1, top1 + rows1 + HALO1)
    own = slice(0, cols1)
    to_right = slice(cols1, cols1 + 128)
    to_left = slice(cols1 + 128, width1)
    for ref, drow, dcol, at_rows, at_cols in (
        (up, -1, 0, above, own),
        (down, 1, 0, below, own),
        (left, 0, -1, beside, to_left),
        (right, 0, 1, beside, to_right),
        (upleft, -1, -1, above, to_left),
        (upright, -1, 1, above, to_right),
        (downleft, 1, -1, below, to_left),
        (downright, 1, 1, below, to_right),
    ):

        @pl.when(neighbour_exists(drow, dcol))
        def _():
            source1[at_rows, at_cols] = ref[...]

    inside1 = col_inside(width1, cols1, 128)
    gain1 = jnp.where(inside1, 0.8 / centre(1), 0.0)
    first_sweep(one, source1, gain1, rows1, HALO1, tiles1)
    sweep(one, two, source1, gain1, rows1, HALO1, 0, tiles1)
    sweep(two, one, source1, gain1, rows1, HALO1, 0, tiles1)

    def residual(tile, start):
        middle, near = neighbours(one, start)
        two[inner(start), :] = source1[inner(start), :] - centre(1) * middle + near

    for_chunks(0, tiles1, residual)
    count1 = 8 * tiles1
    body1 = slice(GUARD, GUARD + count1)
    rows_matrix = pair_rows(144, count1)
    pairs = pair_cols()
    source2 = jnp.concatenate(
        [
            times(apply_rows(rows_matrix, two[body1, 256 * k : 256 * k + 256]), pairs)
            for k in range(width1 // 256)
        ],
        axis=1,
    )
    e2 = coarse_levels(source2, rows1 // 2, cols1 // 2)

    spread, spread_tail = interleave(), interleave_tail()
    near_first = (HALO1 - 8) // 8
    near_count = rows1 + 16
    near_rows = slice(GUARD + HALO1 - 8, GUARD + HALO1 - 8 + near_count)
    matrix = spread_rows(near_count, 96, 8)
    even, odd = spread_cols(e2)
    mask_rows = row_inside(near_count, rows1, 8)
    for k in range(width1 // 256):
        at = slice(256 * k, 256 * k + 256)
        total = one[near_rows, at] + apply_rows(matrix, times(joined(even, odd, k), spread))
        one[near_rows, at] = jnp.where(mask_rows & inside1[:, at], total, 0.0)
    sweep(one, two, source1, gain1, rows1, HALO1, near_first, near_count // 8)
    sweep(two, one, source1, gain1, rows1, HALO1, near_first, near_count // 8)
    sweep(one, two, source1, gain1, rows1, HALO1, near_first, near_count // 8)

    for copy in copies:
        copy.wait()
    rows, cols = image.shape
    width = wide_noisy.shape[1]
    count = rows + 2 * HALO0
    tiles = count // 8
    body0 = slice(GUARD, GUARD + count)
    inside = col_inside(width, cols, 64)
    gain = jnp.where(inside, 0.8 / centre(0), 0.0)
    mask_rows = row_inside(count, rows, HALO0)
    near1 = two[near_rows, :]
    matrix = spread_rows(count, near_count, 4)
    even, odd = spread_cols(near1)

    def add(at, wide):
        total = values[body0, at] + apply_rows(matrix, wide)
        values[body0, at] = jnp.where(mask_rows & inside[:, at], total, 0.0)

    for k in range(cols // 256):
        add(slice(256 * k, 256 * k + 256), times(joined(even, odd, k), spread))
    lane = iota((1, 128), 1)
    last = [jnp.where(lane < 64, x[:, cols1 : cols1 + 128], x[:, cols1 + 128 : width1]) for x in (even, odd)]
    add(slice(cols, width), times(jnp.concatenate(last, axis=1), spread_tail))

    sweep(values, other, source, gain, rows, HALO0, 0, tiles)
    sweep(other, values, source, gain, rows, HALO0, 0, tiles)

    def last_sweep(tile, start):
        middle, near = neighbours(values, start)
        k = chunk_gain(gain, tile, rows, HALO0)
        s = source[inner(start), :]
        e = 0.2 * middle + k * (s + near)
        other[inner(start), :] = e + (wide_noisy[inner(start), :] + 0.25 * s)

    for_chunks(0, tiles, last_sweep)

    half_cols = half_cols_mask(width, cols, 64)

    def dual_step(tile, start, size):
        x = other[pl.ds(start + 8, size + 8), :]
        w = x[0:size]
        half_rows = 0.5 * dual_masks(tile, size, rows, HALO0)
        here = pl.ds(start + 8, size)
        qa = dual_a[here, :] + half_rows * (x[1 : size + 1] - w)
        qb = dual_b[here, :] + half_cols * (east(w) - w)
        a, b = shrunk(qa, qb, wide_strength[here, :])
        return w, a, b

    new_a[8:16, :] = dual_step(0, 0, 8)[1]

    def last_step(tile, start):
        before = new_a[pl.ds(start, 8), :]
        w, a, b = dual_step(tile, start, CHUNK)
        new_a[inner(start), :] = a
        above = jnp.concatenate([before, a], axis=0)[7 : CHUNK + 7]
        d = (a - above) + (b - west(b))
        out = pl.ds(pl.multiple_of(start - 8, 8), CHUNK)
        noisy = wide_noisy[inner(start), :]
        image[out, :] = (0.8 * w + 0.2 * (d + noisy))[:, 0:cols]
        dual[0, out, :] = a[:, 0:cols]
        dual[1, out, :] = b[:, 0:cols]

    parts = written.shape[0]
    size = rows // parts
    sent = []
    for k in range(parts):
        for_chunks(1 + k * size // 8, size // 8, last_step)
        at = pl.ds(k * size, size)
        sent.append(
            pltpu.make_async_copy(image.at[at, :], image_out.at[at, :], written.at[k, 0])
        )
        for c in range(2):
            sent.append(
                pltpu.make_async_copy(
                    dual.at[c, at, :], dual_out.at[c, at, :], written.at[k, 1 + c]
                )
            )
        for copy in sent[-3:]:
            copy.start()
    for copy in sent:
        copy.wait()


def in_vmem(count):
    return [pl.BlockSpec(memory_space=VMEM)] * count


def shapes(*dims):
    return [jax.ShapeDtypeStruct(d, F32) for d in dims]


def from_directions(pieces):
    up_sent, down_sent, left_sent, right_sent, ul, ur, dl, dr = pieces
    return (down_sent, up_sent, right_sent, left_sent, dr, dl, ur, ul)


def per_device(noisy, strength):
    rows, cols = noisy.shape
    sems = [pltpu.SemaphoreType.DMA((8,)), pltpu.SemaphoreType.DMA((8,))]
    pieces = pl.pallas_call(
        exchange_image,
        out_shape=shapes(*[(16, cols)] * 2, *[(32, 128)] * 2, *[(16, 128)] * 4),
        in_specs=in_vmem(2),
        out_specs=in_vmem(8),
        scratch_shapes=[VMEM((2, 16, cols), F32), VMEM((2, 32, 128), F32), VMEM((4, 16, 128), F32)] + sems,
        compiler_params=pltpu.CompilerParams(
            collective_id=0, has_side_effects=True, vmem_limit_bytes=VMEM_LIMIT
        ),
    )(noisy, strength)
    wide = (rows + 2 * HALO0 + 2 * GUARD, cols + 128)
    rows1, cols1 = rows // 2, cols // 2
    *kept, coarse = pl.pallas_call(
        down_level0,
        out_shape=shapes(*[wide] * 6, (rows1, cols1)),
        in_specs=in_vmem(10),
        out_specs=[pl.BlockSpec(memory_space=pl.ANY)] * 6 + in_vmem(1),
        scratch_shapes=[VMEM(wide, F32)] * 7 + [pltpu.SemaphoreType.DMA((6,))],
        compiler_params=pltpu.CompilerParams(vmem_limit_bytes=VMEM_LIMIT),
    )(noisy, strength, *from_directions(pieces))
    pieces = pl.pallas_call(
        exchange_source,
        out_shape=shapes(
            *[(HALO1, cols1)] * 2, *[(rows1, 128)] * 2, *[(HALO1, 128)] * 4
        ),
        in_specs=in_vmem(1),
        out_specs=in_vmem(8),
        scratch_shapes=sems,
        compiler_params=pltpu.CompilerParams(
            collective_id=1, has_side_effects=True, vmem_limit_bytes=VMEM_LIMIT
        ),
    )(coarse)
    wide1 = (rows1 + 2 * HALO1 + 2 * GUARD, cols1 + 256)
    image, dual = pl.pallas_call(
        up_levels,
        out_shape=shapes((rows, cols), (2, rows, cols)),
        in_specs=in_vmem(9) + [pl.BlockSpec(memory_space=pl.ANY)] * 6,
        out_specs=[pl.BlockSpec(memory_space=pl.ANY)] * 2,
        scratch_shapes=[VMEM(wide, F32)] * 6
        + [VMEM(wide1, F32)] * 3
        + [VMEM(wide, F32)] * 2
        + [VMEM((rows, cols), F32), VMEM((2, rows, cols), F32)]
        + [pltpu.SemaphoreType.DMA((6,)), pltpu.SemaphoreType.DMA((4, 3))],
        compiler_params=pltpu.CompilerParams(vmem_limit_bytes=VMEM_LIMIT),
    )(coarse, *from_directions(pieces), *kept)
    return image, dual


def solution(mesh):
    placed = (P("row", "col"), P("row", "col"))
    return jax.shard_map(
        per_device,
        mesh=mesh,
        in_specs=placed,
        out_specs=(P("row", "col"), P(None, "row", "col")),
        check_vma=False,
    )
```

```python
from functools import partial

import jax
import jax.numpy as jnp
from jax import lax
from jax.experimental import pallas as pl
from jax.experimental.pallas import tpu as pltpu
from jax.sharding import PartitionSpec as P

F32 = jnp.float32
BF16 = jnp.bfloat16
MESH = pl.DeviceIdType.MESH
VMEM = pltpu.VMEM

damping = 0.01
GUARD = 8
HALO0 = 8
HALO1 = 72
CHUNK = 16
DIRECTIONS = ((-1, 0), (1, 0), (0, -1), (0, 1), (-1, -1), (-1, 1), (1, -1), (1, 1))
VMEM_LIMIT = 58 * 1024 * 1024


def centre(level):
    return 4.0 + damping * 4.0**level


def iota(shape, dim):
    return lax.broadcasted_iota(jnp.int32, shape, dim)


def west(x):
    return pltpu.roll(x, 1, 1)


def east(x):
    return pltpu.roll(x, x.shape[1] - 1, 1)


def north(x):
    return pltpu.roll(x, 1, 0)


def south(x):
    return pltpu.roll(x, x.shape[0] - 1, 0)


def split(x):
    high = x.astype(BF16)
    return high, (x - high.astype(F32)).astype(BF16)


def times(x, matrix):
    high, low = split(x)
    return jnp.dot(high, matrix, preferred_element_type=F32) + jnp.dot(
        low, matrix, preferred_element_type=F32
    )


def apply_rows(matrix, x):
    high, low = split(x)
    return jnp.dot(matrix, high, preferred_element_type=F32) + jnp.dot(
        matrix, low, preferred_element_type=F32
    )


def as_matrix(mask):
    return jnp.where(mask, 1.0, 0.0).astype(BF16)


def pair_rows(coarse, fine):
    return as_matrix((iota((coarse, fine), 1) >> 1) == iota((coarse, fine), 0))


def pair_cols():
    return as_matrix((iota((256, 128), 0) >> 1) == iota((256, 128), 1))


def pair_cols_tail():
    i = iota((128, 128), 0)
    return as_matrix((i >> 1) + jnp.where(i >= 64, 64, 0) == iota((128, 128), 1))


def interleave():
    i = iota((256, 256), 0)
    return as_matrix(2 * (i & 127) + (i >> 7) == iota((256, 256), 1))


def interleave_tail():
    i = iota((256, 128), 0)
    n = iota((256, 128), 1)
    return as_matrix(2 * (i & 127) + (i >> 7) == n + jnp.where(n >= 64, 128, 0))


def spread_rows(fine, coarse, offset):
    f = iota((fine, coarse), 0)
    k = iota((fine, coarse), 1)
    near = (f >> 1) + offset
    far = near + 2 * (f & 1) - 1
    return (jnp.where(k == near, 0.75, 0.0) + jnp.where(k == far, 0.25, 0.0)).astype(BF16)


def spread_cols(c):
    return 0.75 * c + 0.25 * west(c), 0.75 * c + 0.25 * east(c)


def joined(even, odd, block):
    at = slice(128 * block, 128 * block + 128)
    return jnp.concatenate([even[:, at], odd[:, at]], axis=1)


def col_index(width, own, right):
    lane = iota((1, width), 1)
    return lax.axis_index("col") * own + jnp.where(lane < own + right, lane, lane - width)


def col_inside(width, own, right):
    g = col_index(width, own, right)
    return (g >= 0) & (g < own * lax.axis_size("col"))


def row_inside(count, own, halo):
    g = lax.axis_index("row") * own - halo + iota((count, 1), 0)
    return (g >= 0) & (g < own * lax.axis_size("row"))


def weights(level, count, width, own_rows, own_cols, halo, right):
    inside = row_inside(count, own_rows, halo) & col_inside(width, own_cols, right)
    return jnp.where(inside, 0.8 / centre(level), 0.0)


def neighbour_exists(drow, dcol):
    row = lax.axis_index("row") + drow
    col = lax.axis_index("col") + dcol
    return (
        (row >= 0) & (row < lax.axis_size("row")) & (col >= 0) & (col < lax.axis_size("col"))
    )


def exchange(sources, targets, send_sem, recv_sem):
    barrier = pltpu.get_barrier_semaphore()
    row, col = lax.axis_index("row"), lax.axis_index("col")
    for drow, dcol in DIRECTIONS:

        @pl.when(neighbour_exists(drow, dcol))
        def _():
            pl.semaphore_signal(
                barrier, inc=1, device_id=(row + drow, col + dcol), device_id_type=MESH
            )

    pl.semaphore_wait(
        barrier, sum(jnp.where(neighbour_exists(*d), 1, 0) for d in DIRECTIONS)
    )

    def copy(d):
        drow, dcol = DIRECTIONS[d]
        return pltpu.make_async_remote_copy(
            src_ref=sources[d],
            dst_ref=targets[d],
            send_sem=send_sem.at[d],
            recv_sem=recv_sem.at[d],
            device_id=(row + drow, col + dcol),
            device_id_type=MESH,
        )

    order = (2, 3, 4, 5, 6, 7, 0, 1)
    for d in order:

        @pl.when(neighbour_exists(*DIRECTIONS[d]))
        def _():
            copy(d).start()

    for d in order:
        drow, dcol = DIRECTIONS[d]

        @pl.when(neighbour_exists(drow, dcol))
        def _():
            copy(d).wait_send()

        @pl.when(neighbour_exists(-drow, -dcol))
        def _():
            copy(d).wait_recv()


def exchange_image(
    noisy, strength, *rest
):
    targets, scratch = rest[:8], rest[8:]
    vertical, sides, corners, send_sem, recv_sem = scratch
    rows, cols = noisy.shape
    lane = iota((16, 128), 1)
    for k, ref in enumerate((noisy, strength)):
        at = slice(8 * k, 8 * k + 8)
        vertical[0, at] = ref[0:8, :]
        vertical[1, at] = ref[rows - 8 : rows, :]
        corners[0, at] = ref[0:8, 0:128]
        corners[1, at] = ref[0:8, cols - 128 : cols]
        corners[2, at] = ref[rows - 8 : rows, 0:128]
        corners[3, at] = ref[rows - 8 : rows, cols - 128 : cols]
        first = jnp.zeros((16, 128), F32)
        last = jnp.zeros((16, 128), F32)
        for g in range(16):
            here = (lane >= 8 * g) & (lane < 8 * g + 8)
            near = slice(16 * g, 16 * g + 16)
            first = jnp.where(here, pltpu.roll(ref[near, 0:128], 8 * g, 1), first)
            last = jnp.where(
                here, pltpu.roll(ref[near, cols - 128 : cols], (8 * g + 8) % 128, 1), last
            )
        sides[0, 16 * k : 16 * k + 16] = first
        sides[1, 16 * k : 16 * k + 16] = last
    sources = (
        vertical.at[0],
        vertical.at[1],
        sides.at[0],
        sides.at[1],
        corners.at[0],
        corners.at[1],
        corners.at[2],
        corners.at[3],
    )
    exchange(sources, targets, send_sem, recv_sem)


def exchange_source(source, *rest):
    targets, (send_sem, recv_sem) = rest[:8], rest[8:]
    rows, cols = source.shape
    up, down = pl.ds(0, HALO1), pl.ds(rows - HALO1, HALO1)
    left, right = pl.ds(0, 128), pl.ds(cols - 128, 128)
    sources = (
        source.at[up, :],
        source.at[down, :],
        source.at[:, left],
        source.at[:, right],
        source.at[up, left],
        source.at[up, right],
        source.at[down, left],
        source.at[down, right],
    )
    exchange(sources, targets, send_sem, recv_sem)


def tile_valid(tile, own, halo):
    g = lax.axis_index("row") * own - halo + tile * 8
    return jnp.where((g >= 0) & (g < own * lax.axis_size("row")), 1.0, 0.0)


def chunk_gain(gain, tile, own, halo):
    wide = jnp.broadcast_to(gain, (8, gain.shape[1]))
    return jnp.concatenate(
        [wide * tile_valid(tile + k, own, halo) for k in range(CHUNK // 8)], axis=0
    )


def neighbours(ref, start):
    x = ref[pl.ds(start, CHUNK + 16), :]
    middle = x[8 : CHUNK + 8]
    return middle, (x[7 : CHUNK + 7] + x[9 : CHUNK + 9]) + (west(middle) + east(middle))


def for_chunks(first, tiles, body, unroll=4):
    def step(chunk, carry):
        tile = first + chunk * (CHUNK // 8)
        body(tile, pl.multiple_of(tile * 8, 8))
        return carry

    lax.fori_loop(0, tiles * 8 // CHUNK, step, 0, unroll=unroll)


def inner(start):
    return pl.ds(start + 8, CHUNK)


def sweep(old, new, source, gain, own, halo, first, tiles):
    def body(tile, start):
        middle, beside = neighbours(old, start)
        k = chunk_gain(gain, tile, own, halo)
        new[inner(start), :] = 0.2 * middle + k * (source[inner(start), :] + beside)

    for_chunks(first, tiles, body)


def first_sweep(new, source, gain, own, halo, tiles):
    def body(tile, start):
        k = chunk_gain(gain, tile, own, halo)
        new[inner(start), :] = k * source[inner(start), :]

    for_chunks(0, tiles, body)


def dual_masks(tile, count, own_rows, halo):
    g = lax.axis_index("row") * own_rows - halo + tile * 8 + iota((count, 1), 0)
    return jnp.where((g >= 0) & (g < own_rows * lax.axis_size("row") - 1), 1.0, 0.0)


def shrunk(qa, qb, bound):
    shrink = jnp.minimum(1.0, bound * lax.rsqrt(qa * qa + qb * qb))
    return qa * shrink, qb * shrink


def clear_guards(ref):
    rows, width = ref.shape
    ref[0:GUARD, :] = jnp.zeros((GUARD, width), ref.dtype)
    ref[rows - GUARD : rows, :] = jnp.zeros((GUARD, width), ref.dtype)


def half_cols_mask(width, own, right):
    g = col_index(width, own, right)
    return jnp.where((g >= 0) & (g < own * lax.axis_size("col") - 1), 0.5, 0.0)


def down_level0(
    noisy, strength, up, down, left, right, upleft, upright, downleft, downright,
    *rest,
):
    far, coarse, local, (other, written) = rest[:6], rest[6], rest[7:13], rest[13:]
    wide_noisy, wide_strength, dual_a, dual_b, source, values = local
    copies = [
        pltpu.make_async_copy(local[k], far[k], written.at[k]) for k in range(len(far))
    ]
    rows, cols = noisy.shape
    width = wide_noisy.shape[1]
    total = wide_noisy.shape[0]
    tiles = (total - 2 * GUARD) // 8
    lane = iota((16, 128), 1)
    right_end = jnp.where(neighbour_exists(0, 1), 8, 0)
    left_start = jnp.where(neighbour_exists(0, -1), 120, 128)
    top = GUARD + HALO0
    for k, (ref, wide, fill) in enumerate(((noisy, wide_noisy, 0.0), (strength, wide_strength, 1.0))):
        wide[top : top + rows, 0:cols] = ref[...]
        wide[0:top, :] = jnp.full((top, width), fill, F32)
        wide[top + rows : total, :] = jnp.full((total - top - rows, width), fill, F32)
        from_right = right[16 * k : 16 * k + 16]
        from_left = left[16 * k : 16 * k + 16]
        for g in range(16):
            piece = jnp.where(
                lane < right_end,
                pltpu.roll(from_right, (128 - 8 * g) % 128, 1),
                jnp.where(lane >= left_start, pltpu.roll(from_left, (120 - 8 * g) % 128, 1), fill),
            )
            wide[top + 16 * g : top + 16 * g + 16, cols:width] = piece
        at = slice(8 * k, 8 * k + 8)
        lane8 = lane[0:8]
        for edge, other_left, other_right, drow, place in (
            (up, upleft, upright, -1, GUARD),
            (down, downleft, downright, 1, top + rows),
        ):

            @pl.when(neighbour_exists(drow, 0))
            def _():
                wide[place : place + 8, 0:cols] = edge[at, :]
                wide[place : place + 8, cols:width] = jnp.where(
                    lane8 < right_end,
                    other_right[at, :],
                    jnp.where(lane8 >= left_start, other_left[at, :], fill),
                )

    for ref in (dual_a, dual_b, source, values, other):
        clear_guards(ref)

    inside = col_inside(width, cols, 64)
    gain = jnp.where(inside, 0.8 / centre(0), 0.0)
    half_cols = half_cols_mask(width, cols, 64)

    def first_step(tile, start):
        x = wide_noisy[pl.ds(start + 8, CHUNK + 8), :]
        w = x[0:CHUNK]
        half_rows = 0.5 * dual_masks(tile, CHUNK, rows, HALO0)
        qa = half_rows * (x[1 : CHUNK + 1] - w)
        qb = half_cols * (east(w) - w)
        before = dual_a[pl.ds(start, 8), :]
        a, b = shrunk(qa, qb, wide_strength[inner(start), :])
        dual_a[inner(start), :] = a
        dual_b[inner(start), :] = b
        above = jnp.concatenate([before, a], axis=0)[7 : CHUNK + 7]
        s = 0.8 * ((a - above) + (b - west(b)))
        source[inner(start), :] = s
        values[inner(start), :] = chunk_gain(gain, tile, rows, HALO0) * s

    copies[0].start()
    copies[1].start()
    for_chunks(0, tiles, first_step)
    for copy in copies[2:5]:
        copy.start()
    sweep(values, other, source, gain, rows, HALO0, 0, tiles)
    sweep(other, values, source, gain, rows, HALO0, 0, tiles)

    copies[5].start()

    def residual(tile, start):
        middle, beside = neighbours(values, start)
        other[inner(start), :] = source[inner(start), :] - centre(0) * middle + beside

    for_chunks(1, tiles - 2, residual)
    rows_matrix = pair_rows(rows // 2, rows)
    cols_matrix = pair_cols()
    for block in range(cols // 256):
        piece = other[top : top + rows, 256 * block : 256 * block + 256]
        coarse[:, 128 * block : 128 * block + 128] = times(
            apply_rows(rows_matrix, piece), cols_matrix
        )
    for copy in copies:
        copy.wait()


def relax(e, source, gain):
    beside = (north(e) + south(e)) + (west(e) + east(e))
    return 0.2 * e + gain * (source + beside)


def smoothed(source, gain):
    e = gain * source
    e = relax(e, source, gain)
    return relax(e, source, gain)


def remaining(e, source, level):
    return source - centre(level) * e + ((north(e) + south(e)) + (west(e) + east(e)))


def coarse_levels(source2, own_rows, own_cols):
    n2, n3, n4 = 144, 80, 48
    gain2 = weights(2, n2, own_cols + 128, own_rows, own_cols, 36, 64)
    gain3 = weights(3, n3, 256, own_rows // 2, own_cols // 2, 18, 64)
    gain4 = weights(4, n4, 128, own_rows // 4, own_cols // 4, 9, 32)
    spread, spread_tail = interleave(), interleave_tail()
    pairs, pairs_tail = pair_cols(), pair_cols_tail()

    e2 = smoothed(source2, gain2)
    left = apply_rows(pair_rows(n3, n2), remaining(e2, source2, 2))
    source3 = jnp.concatenate(
        [times(left[:, 0:256], pairs), times(left[:, 256:384], pairs_tail)], axis=1
    )
    e3 = smoothed(source3, gain3)
    source4 = times(apply_rows(pair_rows(n4, n3), remaining(e3, source3, 3)), pairs)
    e4 = smoothed(source4, gain4)

    even, odd = spread_cols(e4)
    wide = times(joined(even, odd, 0), spread)
    e3 = e3 + apply_rows(spread_rows(n3, n4, 0), wide)
    e3 = jnp.where(gain3 > 0.0, e3, 0.0)
    for _ in range(3):
        e3 = relax(e3, source3, gain3)

    even, odd = spread_cols(e3)
    wide = jnp.concatenate(
        [times(joined(even, odd, 0), spread), times(joined(even, odd, 1), spread_tail)], axis=1
    )
    kept = slice(24, 120)
    e2, source2, gain2 = e2[kept], source2[kept], gain2[kept]
    e2 = e2 + apply_rows(spread_rows(96, n3, 12), wide)
    e2 = jnp.where(gain2 > 0.0, e2, 0.0)
    for _ in range(3):
        e2 = relax(e2, source2, gain2)
    return e2


def up_levels(
    coarse, up, down, left, right, upleft, upright, downleft, downright,
    *rest,
):
    far, (image_out, dual_out), local = rest[:6], rest[6:8], rest[8:14]
    source1, one, two, other, new_a, image, dual, fetched, written = rest[14:]
    wide_noisy, wide_strength, dual_a, dual_b, source, values = local
    copies = [
        pltpu.make_async_copy(far[k], local[k], fetched.at[k]) for k in range(len(far))
    ]
    for copy in copies:
        copy.start()
    rows1, cols1 = coarse.shape
    width1 = cols1 + 256
    tiles1 = (source1.shape[0] - 2 * GUARD) // 8
    top1 = GUARD + HALO1
    source1[...] = jnp.zeros(source1.shape, F32)
    for ref in (one, two, other, new_a):
        clear_guards(ref)
    source1[top1 : top1 + rows1, 0:cols1] = coarse[...]
    above = slice(GUARD, top1)
    beside = slice(top1, top1 + rows1)
    below = slice(top1 + rows1, top1 + rows1 + HALO1)
    own = slice(0, cols1)
    to_right = slice(cols1, cols1 + 128)
    to_left = slice(cols1 + 128, width1)
    for ref, drow, dcol, at_rows, at_cols in (
        (up, -1, 0, above, own),
        (down, 1, 0, below, own),
        (left, 0, -1, beside, to_left),
        (right, 0, 1, beside, to_right),
        (upleft, -1, -1, above, to_left),
        (upright, -1, 1, above, to_right),
        (downleft, 1, -1, below, to_left),
        (downright, 1, 1, below, to_right),
    ):

        @pl.when(neighbour_exists(drow, dcol))
        def _():
            source1[at_rows, at_cols] = ref[...]

    inside1 = col_inside(width1, cols1, 128)
    gain1 = jnp.where(inside1, 0.8 / centre(1), 0.0)
    first_sweep(one, source1, gain1, rows1, HALO1, tiles1)
    sweep(one, two, source1, gain1, rows1, HALO1, 0, tiles1)
    sweep(two, one, source1, gain1, rows1, HALO1, 0, tiles1)

    def residual(tile, start):
        middle, near = neighbours(one, start)
        two[inner(start), :] = source1[inner(start), :] - centre(1) * middle + near

    for_chunks(0, tiles1, residual)
    count1 = 8 * tiles1
    body1 = slice(GUARD, GUARD + count1)
    rows_matrix = pair_rows(144, count1)
    pairs = pair_cols()
    source2 = jnp.concatenate(
        [
            times(apply_rows(rows_matrix, two[body1, 256 * k : 256 * k + 256]), pairs)
            for k in range(width1 // 256)
        ],
        axis=1,
    )
    e2 = coarse_levels(source2, rows1 // 2, cols1 // 2)

    spread, spread_tail = interleave(), interleave_tail()
    near_first = (HALO1 - 8) // 8
    near_count = rows1 + 16
    near_rows = slice(GUARD + HALO1 - 8, GUARD + HALO1 - 8 + near_count)
    matrix = spread_rows(near_count, 96, 8)
    even, odd = spread_cols(e2)
    mask_rows = row_inside(near_count, rows1, 8)
    for k in range(width1 // 256):
        at = slice(256 * k, 256 * k + 256)
        total = one[near_rows, at] + apply_rows(matrix, times(joined(even, odd, k), spread))
        one[near_rows, at] = jnp.where(mask_rows & inside1[:, at], total, 0.0)
    sweep(one, two, source1, gain1, rows1, HALO1, near_first, near_count // 8)
    sweep(two, one, source1, gain1, rows1, HALO1, near_first, near_count // 8)
    sweep(one, two, source1, gain1, rows1, HALO1, near_first, near_count // 8)

    for copy in copies:
        copy.wait()
    rows, cols = image.shape
    width = wide_noisy.shape[1]
    count = rows + 2 * HALO0
    tiles = count // 8
    body0 = slice(GUARD, GUARD + count)
    inside = col_inside(width, cols, 64)
    gain = jnp.where(inside, 0.8 / centre(0), 0.0)
    mask_rows = row_inside(count, rows, HALO0)
    near1 = two[near_rows, :]
    matrix = spread_rows(count, near_count, 4)
    even, odd = spread_cols(near1)

    def add(at, wide):
        total = values[body0, at] + apply_rows(matrix, wide)
        values[body0, at] = jnp.where(mask_rows & inside[:, at], total, 0.0)

    for k in range(cols // 256):
        add(slice(256 * k, 256 * k + 256), times(joined(even, odd, k), spread))
    lane = iota((1, 128), 1)
    last = [jnp.where(lane < 64, x[:, cols1 : cols1 + 128], x[:, cols1 + 128 : width1]) for x in (even, odd)]
    add(slice(cols, width), times(jnp.concatenate(last, axis=1), spread_tail))

    sweep(values, other, source, gain, rows, HALO0, 0, tiles)
    sweep(other, values, source, gain, rows, HALO0, 0, tiles)

    def last_sweep(tile, start):
        middle, near = neighbours(values, start)
        k = chunk_gain(gain, tile, rows, HALO0)
        s = source[inner(start), :]
        e = 0.2 * middle + k * (s + near)
        other[inner(start), :] = e + (wide_noisy[inner(start), :] + 0.25 * s)

    for_chunks(0, tiles, last_sweep)

    half_cols = half_cols_mask(width, cols, 64)

    def dual_step(tile, start, size):
        x = other[pl.ds(start + 8, size + 8), :]
        w = x[0:size]
        half_rows = 0.5 * dual_masks(tile, size, rows, HALO0)
        here = pl.ds(start + 8, size)
        qa = dual_a[here, :] + half_rows * (x[1 : size + 1] - w)
        qb = dual_b[here, :] + half_cols * (east(w) - w)
        a, b = shrunk(qa, qb, wide_strength[here, :])
        return w, a, b

    new_a[8:16, :] = dual_step(0, 0, 8)[1]

    def last_step(tile, start):
        before = new_a[pl.ds(start, 8), :]
        w, a, b = dual_step(tile, start, CHUNK)
        new_a[inner(start), :] = a
        above = jnp.concatenate([before, a], axis=0)[7 : CHUNK + 7]
        d = (a - above) + (b - west(b))
        out = pl.ds(pl.multiple_of(start - 8, 8), CHUNK)
        noisy = wide_noisy[inner(start), :]
        image[out, :] = (0.8 * w + 0.2 * (d + noisy))[:, 0:cols]
        dual[0, out, :] = a[:, 0:cols]
        dual[1, out, :] = b[:, 0:cols]

    parts = written.shape[0]
    size = rows // parts
    sent = []
    for k in range(parts):
        for_chunks(1 + k * size // 8, size // 8, last_step)
        at = pl.ds(k * size, size)
        sent.append(
            pltpu.make_async_copy(image.at[at, :], image_out.at[at, :], written.at[k, 0])
        )
        for c in range(2):
            sent.append(
                pltpu.make_async_copy(
                    dual.at[c, at, :], dual_out.at[c, at, :], written.at[k, 1 + c]
                )
            )
        for copy in sent[-3:]:
            copy.start()
    for copy in sent:
        copy.wait()


def in_vmem(count):
    return [pl.BlockSpec(memory_space=VMEM)] * count


def shapes(*dims):
    return [jax.ShapeDtypeStruct(d, F32) for d in dims]


def from_directions(pieces):
    up_sent, down_sent, left_sent, right_sent, ul, ur, dl, dr = pieces
    return (down_sent, up_sent, right_sent, left_sent, dr, dl, ur, ul)


def per_device(noisy, strength):
    rows, cols = noisy.shape
    sems = [pltpu.SemaphoreType.DMA((8,)), pltpu.SemaphoreType.DMA((8,))]
    pieces = pl.pallas_call(
        exchange_image,
        out_shape=shapes(*[(16, cols)] * 2, *[(32, 128)] * 2, *[(16, 128)] * 4),
        in_specs=in_vmem(2),
        out_specs=in_vmem(8),
        scratch_shapes=[VMEM((2, 16, cols), F32), VMEM((2, 32, 128), F32), VMEM((4, 16, 128), F32)] + sems,
        compiler_params=pltpu.CompilerParams(
            collective_id=0, has_side_effects=True, vmem_limit_bytes=VMEM_LIMIT
        ),
    )(noisy, strength)
    wide = (rows + 2 * HALO0 + 2 * GUARD, cols + 128)
    rows1, cols1 = rows // 2, cols // 2
    *kept, coarse = pl.pallas_call(
        down_level0,
        out_shape=shapes(*[wide] * 6, (rows1, cols1)),
        in_specs=in_vmem(10),
        out_specs=[pl.BlockSpec(memory_space=pl.ANY)] * 6 + in_vmem(1),
        scratch_shapes=[VMEM(wide, F32)] * 7 + [pltpu.SemaphoreType.DMA((6,))],
        compiler_params=pltpu.CompilerParams(vmem_limit_bytes=VMEM_LIMIT),
    )(noisy, strength, *from_directions(pieces))
    pieces = pl.pallas_call(
        exchange_source,
        out_shape=shapes(
            *[(HALO1, cols1)] * 2, *[(rows1, 128)] * 2, *[(HALO1, 128)] * 4
        ),
        in_specs=in_vmem(1),
        out_specs=in_vmem(8),
        scratch_shapes=sems,
        compiler_params=pltpu.CompilerParams(
            collective_id=1, has_side_effects=True, vmem_limit_bytes=VMEM_LIMIT
        ),
    )(coarse)
    wide1 = (rows1 + 2 * HALO1 + 2 * GUARD, cols1 + 256)
    image, dual = pl.pallas_call(
        up_levels,
        out_shape=shapes((rows, cols), (2, rows, cols)),
        in_specs=in_vmem(9) + [pl.BlockSpec(memory_space=pl.ANY)] * 6,
        out_specs=[pl.BlockSpec(memory_space=pl.ANY)] * 2,
        scratch_shapes=[VMEM(wide, F32)] * 6
        + [VMEM(wide1, F32)] * 3
        + [VMEM(wide, F32)] * 2
        + [VMEM((rows, cols), F32), VMEM((2, rows, cols), F32)]
        + [pltpu.SemaphoreType.DMA((6,)), pltpu.SemaphoreType.DMA((4, 3))],
        compiler_params=pltpu.CompilerParams(vmem_limit_bytes=VMEM_LIMIT),
    )(coarse, *from_directions(pieces), *kept)
    return image, dual


def solution(mesh):
    placed = (P("row", "col"), P("row", "col"))
    return jax.shard_map(
        per_device,
        mesh=mesh,
        in_specs=placed,
        out_specs=(P("row", "col"), P(None, "row", "col")),
        check_vma=False,
    )
```
